512 devices in a mesh: row: 64 (over z, y_lo, core), grp: 8 (over y_hi, x).
Axes of the slice: x: 4, y: 4 (y_hi: 2, y_lo: 2; y = y_hi * 2 + y_lo), z: 16, core: 2. Of those that a mesh axis runs over, the one named last changes fastest.
Arguments:
- tokens: bfloat16 [128, 256, 1024], P('row', None, 'grp')
- spec_first: float32 [2, 1024, 128], P(None, 'grp'), may hold values from -0.5 to 0.5
- spec_second: float32 [2, 1024, 128], P(None, 'grp')
- up_weight: bfloat16 [1024, 4096], P(None, 'grp'), may hold values from -0.1875 to 0.1875
- down_weight: bfloat16 [4096, 1024], P('grp'), may hold values from -0.09375 to 0.09375
- head_weight: bfloat16 [1024, 128], P('grp'), may hold values from -0.1875 to 0.1875
- ocean_vel: float32 [2, 1024, 2048], P(None, 'row', 'grp'), may hold values from -4 to 4
- land_mask: int32 [1024, 2048], P('row', 'grp'), may hold values 0 or 1
- ice_mask: int32 [1024, 2048], P('row', 'grp'), may hold values 0 or 1
Outputs:
- block_out: bfloat16 [128, 256, 1024], P('row', None, 'grp')
- ocean_next: float32 [2, 1024, 2048], P(None, 'row', 'grp')
The draws below stay inside these ranges and needn't reach their ends.
All inputs are finite; a program needn't handle non-finite values. No bound on the sum of `land_mask` or of `ice_mask` on one device may be relied on, other than what follows from the above.
Results may differ from the reference program's by a relative error of at most 0.0085.
Values may be sent and summed in bfloat16 or wider, within the bound.
A program may use at most 64 MiB of HBM per device.

```python
import math
import jax
import jax.numpy as jnp
from jax import lax

EMBED = 1024
FF = 4096
BLOCKS = 8
BLOCK_SIZE = 128
W = 256
PATCH = 8
H = 128
HP = 1024
WP = 2048
N_GRP = 8


def draw_tokens(key, part):
    key = jax.random.fold_in(key, 11)
    key_base, key_chan, key_row = jax.random.split(key, 3)
    ramp = jnp.exp(math.log(3.0) * jnp.arange(EMBED, dtype=jnp.float32) / EMBED)
    chan_scale = 0.15 * ramp * jnp.exp(jax.random.uniform(key_chan, (EMBED,), jnp.float32, -0.55, 0.55))
    row_scale = jnp.exp(jax.random.uniform(key_row, (H, W, 1), jnp.float32, -0.7, 0.7))
    base_vals = jax.random.normal(key_base, (H, W, EMBED), jnp.float32)
    return (base_vals * chan_scale * row_scale).astype(jnp.bfloat16)


def draw_spec_second(key, part):
    key = jax.random.fold_in(key, 23)
    raw_vals = jax.random.normal(key, (2, BLOCKS, BLOCK_SIZE, BLOCK_SIZE), jnp.float32) * BLOCK_SIZE ** (-0.5)
    column_mean = jnp.mean(raw_vals, axis=2, keepdims=True)
    centered = raw_vals - 0.9 * column_mean
    return centered.reshape(2, EMBED, BLOCK_SIZE).astype(jnp.float32)


def with_ends(values, rng, smallest, largest):
    shape = values.shape
    spot = [jax.random.randint(jax.random.fold_in(rng, axis), (), 0, shape[axis]) for axis in range(len(shape))]
    values = values.at[tuple(spot)].set(smallest)
    longest = shape.index(max(shape))
    spot[longest] = (spot[longest] + 1) % shape[longest]
    return values.at[tuple(spot)].set(largest)


def shard_levels(own_key, shape, cuts, smallest, high):
    gain = 1.0
    for axis_at, parts in cuts:
        heights = jax.random.uniform(jax.random.fold_in(jax.random.fold_in(own_key, 6), axis_at), (parts,), jnp.float32, smallest / len(cuts), high / len(cuts))
        gain = gain * jnp.repeat(jnp.exp(heights), shape[axis_at] // parts).reshape((-1,) + (1,) * (len(shape) - 1 - axis_at))
    return gain


def normal_values(key, extent, deviation, reach, shards=(), kind=jnp.bfloat16):
    level = shard_levels(key, extent, shards, -0.22, 0.18) if shards else 1.0
    array = jax.random.normal(key, extent, jnp.float32) * deviation * level
    return jnp.minimum(jnp.maximum(array, -reach), reach).astype(kind)


def setup_inputs(seed: int = 0) -> dict:
    seeds = jax.random.split(jax.random.key(seed), 10)
    return {
        "tokens": draw_tokens(jax.random.fold_in(seeds[9], 71), 0),
        "spec_first": normal_values(seeds[1], (2, EMBED, BLOCK_SIZE), BLOCK_SIZE ** -0.5, 0.5, ((1, 8),), jnp.float32),
        "spec_second": draw_spec_second(jax.random.fold_in(seeds[9], 71), 0),
        "up_weight": normal_values(seeds[3], (EMBED, FF), EMBED ** -0.5, 0.1875, ((1, 8),)),
        "down_weight": normal_values(seeds[4], (FF, EMBED), FF ** -0.5, 0.09375, ((0, 8),)),
        "head_weight": normal_values(seeds[5], (EMBED, 2 * PATCH * PATCH), EMBED ** -0.5, 0.1875, ((0, 8),)),
        "ocean_vel": normal_values(seeds[6], (2, HP, WP), 1.0, 4.0, ((1, 64), (2, 8)), jnp.float32),
        "land_mask": with_ends((jax.random.randint(seeds[7], (HP, WP), 0, 5) < 4).astype(jnp.int32), jax.random.fold_in(seeds[7], 1), 0, 1),
        "ice_mask": with_ends((jax.random.randint(seeds[8], (HP, WP), 0, 3) < 2).astype(jnp.int32), jax.random.fold_in(seeds[8], 1), 0, 1),
    }


highest = lax.Precision.HIGHEST
epsilon = 1e-05
shrink_level = 0.01
drag_coef = 0.25
time_step = 0.5
coriolis = 0.3
viscosity = 1.0
speed_floor = 0.01

def layer_norm(values):
    channels = values.shape[-1]
    first = lax.optimization_barrier(jnp.sum(values, axis=-1, keepdims=True)) / channels
    second = lax.optimization_barrier(jnp.sum(values * values, axis=-1, keepdims=True)) / channels
    return (values - first) * lax.rsqrt(second - first * first + epsilon)

def soft_shrink(values):
    return values - jnp.clip(values, -shrink_level, shrink_level)

def block_mix(real_part, imag_part, spec_first, spec_second, block_size):
    base_shape = real_part.shape
    local_blocks = base_shape[-1] // block_size
    real_part = real_part.reshape(base_shape[:-1] + (local_blocks, block_size))
    imag_part = imag_part.reshape(base_shape[:-1] + (local_blocks, block_size))
    first = spec_first.reshape(2, local_blocks, block_size, block_size)
    second = spec_second.reshape(2, local_blocks, block_size, block_size)

    def apply_block(values, matrix):
        return jnp.einsum('qkbi,bij->qkbj', values, matrix, precision=highest)
    hid_real = jax.nn.relu(apply_block(real_part, first[0]) - apply_block(imag_part, first[1]))
    hid_imag = jax.nn.relu(apply_block(real_part, first[1]) + apply_block(imag_part, first[0]))
    out_real = soft_shrink(apply_block(hid_real, second[0]) - apply_block(hid_imag, second[1]))
    out_imag = soft_shrink(apply_block(hid_real, second[1]) + apply_block(hid_imag, second[0]))
    return (out_real.reshape(base_shape), out_imag.reshape(base_shape))

def reference(tokens, spec_first, spec_second, up_weight, down_weight, head_weight, ocean_vel, land_mask, ice_mask):
    inputs = tokens.astype(jnp.float32)
    normed = layer_norm(inputs)
    spectra = jnp.fft.rfft2(normed, axes=(0, 1), norm='ortho')[:, :W // 2]
    mix_real, mix_imag = block_mix(jnp.real(spectra), jnp.imag(spectra), spec_first, spec_second, BLOCK_SIZE)
    zero_col = jnp.zeros((H, 1, EMBED), mix_real.dtype)
    full = lax.complex(jnp.concatenate([mix_real, zero_col], axis=1), jnp.concatenate([mix_imag, zero_col], axis=1))
    filtered = jnp.fft.irfft2(full, s=(H, W), axes=(0, 1), norm='ortho')
    mixed_in = (inputs + normed + filtered).reshape(H * W, EMBED)
    normed_two = layer_norm(mixed_in).astype(jnp.bfloat16)
    hidden = jax.nn.gelu(jnp.dot(normed_two, up_weight, preferred_element_type=jnp.float32), approximate=False).astype(jnp.bfloat16)
    hidden_width = FF // N_GRP
    summed = jnp.zeros((H * W, EMBED), jnp.float32)
    for group in range(N_GRP):
        partial_value = jnp.dot(hidden[:, group * hidden_width:(group + 1) * hidden_width], down_weight[group * hidden_width:(group + 1) * hidden_width], preferred_element_type=jnp.float32)
        rounded = lax.optimization_barrier(partial_value.astype(jnp.bfloat16))
        summed = summed + rounded.astype(jnp.float32)
    block_out = (mixed_in + summed).astype(jnp.bfloat16)
    velocity = jnp.dot(block_out, head_weight, preferred_element_type=jnp.float32)
    ice_vel = velocity.reshape(H, W, 2, PATCH, PATCH).transpose(2, 0, 3, 1, 4).reshape(2, H * PATCH, W * PATCH)
    land_open = land_mask.astype(jnp.float32)
    ice_cover = ice_mask.astype(jnp.float32)
    ocean_now = ocean_vel * land_open[None]
    padded = jnp.pad(ocean_now, ((0, 0), (1, 1), (1, 1)))
    center = padded[:, 1:-1, 1:-1]
    laplace = padded[:, 2:, 1:-1] + padded[:, :-2, 1:-1] + padded[:, 1:-1, 2:] + padded[:, 1:-1, :-2] - 4.0 * center
    relative = ice_vel - ocean_now
    drift_speed = jnp.sqrt(relative[0] * relative[0] + relative[1] * relative[1] + speed_floor)
    stress = drag_coef * (ice_cover * drift_speed)[None] * relative
    rotated = jnp.stack([ocean_now[1], -ocean_now[0]])
    ocean_next = land_open[None] * (ocean_now + time_step * (coriolis * rotated + stress + viscosity * laplace))
    return (block_out.reshape(H, W, EMBED), ocean_next)
```

```python
import functools
import math

import jax
import jax.numpy as jnp
import ml_dtypes
import numpy as np
from jax import lax
from jax.experimental import pallas as pl
from jax.experimental.pallas import tpu as pltpu
from jax.sharding import PartitionSpec as P

PATCH = 8
C = 128

epsilon = 1e-05
shrink_level = 0.01
drag_coef = 0.25
time_step = 0.5
coriolis = 0.3
viscosity = 1.0
speed_floor = 0.01

F32 = jnp.float32
BF16 = jnp.bfloat16
MESH = pl.DeviceIdType.MESH


def dft_tables(planes):
    height, width = 8 * planes, 16 * planes
    size = 16 * planes
    row = np.arange(size)
    k, part = row // 2, row % 2
    angle = 2.0 * np.pi * ((k[:, None] * np.arange(width)[None, :]) % width) / width
    row_fwd = np.where(part[:, None] == 0, np.cos(angle), -np.sin(angle))
    row_bwd = np.where(k == 0, 1.0, 2.0)[None, :] * row_fwd.T
    regroup = np.zeros((size, size))
    at = 0
    for q in range(4):
        for kk in range(2):
            for z in range(planes):
                for part_at in range(2):
                    regroup[at, z * 16 + (2 * q + kk) * 2 + part_at] = 1.0
                    at += 1
    col = np.array(
        [(8 * z + 2 * q + r, p) for r in range(2) for q in range(4) for z in range(planes) for p in range(2)]
    )
    col_h, col_part = col[:, 0], col[:, 1]
    angle = 2.0 * np.pi * ((np.arange(height)[:, None] * col_h[None, :]) % height) / height
    cos, sin = np.cos(angle), np.sin(angle)
    real = np.where(col_part[None, :] == 0, cos, sin)
    imag = np.where(col_part[None, :] == 0, -sin, cos)
    col_fwd = np.concatenate([real, imag], axis=0)
    tables = [row_fwd, regroup, col_fwd, col_fwd.T, regroup.T, row_bwd]
    return np.concatenate(tables, axis=0).astype(ml_dtypes.bfloat16)


def dot(a, b):
    return jnp.dot(a, b, preferred_element_type=F32)


def dot_nt(a, b):
    return lax.dot_general(a, b, (((1,), (1,)), ((), ())), preferred_element_type=F32)


def split_hi_lo(values):
    hi = values.astype(BF16)
    return hi, (values - hi.astype(F32)).astype(BF16)


def soft_shrink(values):
    return values - jnp.clip(values, -shrink_level, shrink_level)


def gelu(values):
    return 0.5 * values * (1.0 + lax.erf(values * (1.0 / math.sqrt(2.0))))


def far_first(count):
    return sorted(range(1, count), key=lambda i: -min(i, count - i))


def complex_matrix(ref):
    real, imag = ref[0], ref[1]
    top = jnp.concatenate([real, imag], axis=1)
    low = jnp.concatenate([-imag, real], axis=1)
    return jnp.concatenate([top, low], axis=0)


def stack_rows(rows, count, width):
    at = lax.broadcasted_iota(jnp.int32, (count, width), 0)
    out = jnp.zeros((count, width), F32)
    for i, values in enumerate(rows):
        out = jnp.where(at == i, values, out)
    return out


def columns_of(rows, width):
    top = stack_rows(rows, 8, width)
    return jnp.concatenate([top, jnp.zeros((C - 8, width), F32)], axis=0).T


def kernel(
    planes,
    groups,
    tok_hbm, first_hbm, second_hbm, up_hbm, down_hbm, head_hbm, vel_hbm, land_hbm, ice_hbm, tab_hbm,
    bo_hbm, oc_hbm,
    tok, first, second, up, down, head, vel, land, ice, tab,
    st1_send, st1_recv, z1_send, z1_recv, p1_send, p1_recv, p2_send, p2_recv, z2_send, z2_recv,
    mixed, y_send, y_recv, st2_send, st2_recv, peer_up, peer_down, hid_own, hid_peer, rs_send, rs_recv,
    bo, bo_recv, hw_send, hw_recv, now, halo_up, halo_down, halo_left, halo_right, ocean,
    local_sem, send_sem, recv_sem, out_sem,
):
    width = tok.shape[1]
    across = groups // 2
    total_channels = C * groups
    row, grp = lax.axis_index("row"), lax.axis_index("grp")
    rows = 4 * planes
    z, q = row // 4, row % 4
    y_lo, core = q // 2, q % 2
    y_hi, x = grp // across, grp % across
    hidden = up.shape[1]

    loads = {}
    for i, (name, src, dst) in enumerate(
        [
            ("tok", tok_hbm, tok),
            ("tab", tab_hbm, tab),
            ("vel", vel_hbm, vel),
            ("land", land_hbm, land),
            ("head", head_hbm, head),
            ("first", first_hbm, first),
            ("second", second_hbm, second),
            ("up", up_hbm, up),
            ("down", down_hbm, down),
            ("ice", ice_hbm, ice),
        ]
    ):
        loads[name] = pltpu.make_async_copy(src, dst, local_sem.at[i])
        loads[name].start()

    z_peers = [(lax.rem(z + i, planes) * 4 + q, grp) for i in far_first(planes)]
    q_peers = [(z * 4 + (q + i) % 4, grp) for i in (2, 3, 1)]
    g_peers = [lax.rem(grp + i, groups) for i in far_first(groups)]
    row_above, row_below = lax.rem(row + rows - 1, rows), lax.rem(row + 1, rows)
    weight_peer = (z * 4 + (1 - y_lo) * 2 + core, (1 - y_hi) * across + x)
    sibling = (z * 4 + y_lo * 2 + (1 - core), grp)
    greeted = z_peers + q_peers + [(row, g) for g in g_peers]
    greeted += [(row_above, grp), (row_below, grp), weight_peer]
    barrier = pltpu.get_barrier_semaphore()
    for peer in greeted:
        pl.semaphore_signal(barrier, inc=1, device_id=peer, device_id_type=MESH)

    ones = jnp.ones((16, C), BF16)
    loads["tok"].wait()
    sums = []
    squares = []
    for r in range(2):
        values = tok[r]
        wide = values.astype(F32)
        hi, lo = split_hi_lo(wide * wide)
        sums.append(dot_nt(ones, values)[0:1])
        squares.append((dot_nt(ones, hi) + dot_nt(ones, lo))[0:1])
    st1_send[...] = stack_rows(sums + squares, 8, width)
    st1_recv[grp] = st1_send[...]
    loads["head"].wait()
    hw_send[...] = head[...].astype(F32).T.astype(BF16)
    hw_recv[grp] = hw_send[...]
    loads["vel"].wait()
    loads["land"].wait()
    open_water = land[...].astype(F32)
    now[0] = vel[0] * open_water
    now[1] = vel[1] * open_water

    pl.semaphore_wait(barrier, len(greeted))

    drains = []

    def send(src, dst, at, peer):
        pltpu.make_async_remote_copy(
            src_ref=src,
            dst_ref=dst,
            send_sem=send_sem.at[at],
            recv_sem=recv_sem.at[at],
            device_id=peer,
            device_id_type=MESH,
        ).start()

    def wait_on(sem, like):
        pltpu.make_async_copy(like, like, sem).wait()

    def arrived(at, like):
        wait_on(recv_sem.at[at], like)
        drains.append((at, like))

    ST1, WUP, WDN, HW, HUP, HDN, HLF, HRT, Z1, P1, P2, Z2, Y, ST2, FUP, FDN, RS, BO = range(18)

    for g in g_peers:
        send(st1_send, st1_recv.at[grp], ST1, (row, g))
    half_up = pl.ds(pl.multiple_of(core * (up.shape[0] // 2), up.shape[0] // 2), up.shape[0] // 2)
    half_dn = pl.ds(pl.multiple_of(core * (hidden // 2), hidden // 2), hidden // 2)
    send(up_hbm.at[half_up], peer_up.at[half_up], WUP, weight_peer)
    send(down_hbm.at[half_dn], peer_down.at[half_dn], WDN, weight_peer)

    arrived(ST1, st1_recv.at[pl.ds(0, groups - 1)])
    totals = st1_recv[0]
    for g in range(1, groups):
        totals = totals + st1_recv[g]
    totals = totals / total_channels
    mean, mean_square = totals[0:2], totals[2:4]
    scale = lax.rsqrt(mean_square - mean * mean + epsilon)
    stats = columns_of([mean[0:1], mean[1:2], scale[0:1], scale[1:2]], width)
    loads["tab"].wait()
    size = 16 * planes

    def table(i):
        return tab[i * size : (i + 1) * size]

    normed = []
    for r in range(2):
        inputs = tok[r].astype(F32)
        normed.append((inputs - stats[:, r : r + 1]) * stats[:, 2 + r : 3 + r])
        mixed[r] = inputs + normed[r]

    flat = jnp.concatenate([normed[0].astype(BF16), normed[1].astype(BF16)], axis=1)
    row_scale, col_scale = 1.0 / math.sqrt(width), 1.0 / math.sqrt(8 * planes)
    z1_send[...] = (dot(table(0), flat) * row_scale).astype(BF16).reshape(planes, 16, 2 * C)
    for peer in z_peers:
        send(z1_send.at[peer[0] // 4], z1_recv.at[z], Z1, peer)
    z1_recv[z] = z1_send[z]

    for g in g_peers:
        send(hw_send, hw_recv.at[grp], HW, (row, g))
    send(now.at[:, pl.ds(8, 8)], halo_up, HUP, (row_below, grp))
    send(now.at[:, pl.ds(0, 8)], halo_down, HDN, (row_above, grp))
    lanes = now.shape[2]
    send(now.at[:, :, pl.ds(lanes - C, C)], halo_left, HLF, (row, lax.rem(grp + 1, groups)))
    send(now.at[:, :, pl.ds(0, C)], halo_right, HRT, (row, lax.rem(grp + groups - 1, groups)))
    loads["first"].wait()
    loads["second"].wait()
    weight_one = complex_matrix(first).astype(BF16)
    weight_two, weight_two_lo = split_hi_lo(complex_matrix(second))
    loads["up"].wait()
    loads["down"].wait()
    loads["ice"].wait()
    block_at = lax.broadcasted_iota(jnp.int32, (16, total_channels), 0)
    block_of = lax.broadcasted_iota(jnp.int32, (16, total_channels), 1) // C
    pick = jnp.where(block_at == block_of, 1.0, 0.0).astype(BF16)

    def column_sums(weights):
        sums = dot(pick, weights)
        hi, lo = split_hi_lo(sums)
        pad = jnp.zeros((C - 16, hidden), BF16)
        return jnp.concatenate([hi, pad], axis=0), jnp.concatenate([lo, pad], axis=0)

    own_sums = column_sums(up[...])

    arrived(Z1, z1_recv.at[pl.ds(0, planes - 1)])
    quarter = 4 * planes
    p1_send[...] = dot(table(1), z1_recv[...].reshape(size, 2 * C)).astype(BF16).reshape(4, quarter, 2 * C)
    for peer in q_peers:
        send(p1_send.at[peer[0] % 4], p1_recv.at[q], P1, peer)
    p1_recv[q] = p1_send[q]
    arrived(P1, p1_recv.at[pl.ds(0, 3)])

    half = 2 * planes

    def gathered(kk, r):
        return [p1_recv[q_at, kk * half : (kk + 1) * half, r * C : (r + 1) * C] for q_at in range(4)]

    by_kk = [jnp.concatenate(gathered(kk, 0) + gathered(kk, 1), axis=0) for kk in range(2)]
    freq = (dot(table(2), jnp.concatenate(by_kk, axis=1)) * col_scale).astype(BF16)
    height = 8 * planes

    def swapped(values):
        top = jnp.concatenate([values[:height, :C], values[height:, :C]], axis=1)
        low = jnp.concatenate([values[:height, C:], values[height:, C:]], axis=1)
        return jnp.concatenate([top, low], axis=0)

    hid = jax.nn.relu(dot(swapped(freq), weight_one)).astype(BF16)
    mix = soft_shrink(dot(hid, weight_two) + dot(hid, weight_two_lo)).astype(BF16)
    back = (dot(table(3), swapped(mix)) * col_scale).astype(BF16)
    for q_at in range(4):
        for r in range(2):
            for kk in range(2):
                start = r * height + q_at * half
                p2_send[q_at, kk * half : (kk + 1) * half, r * C : (r + 1) * C] = back[
                    start : start + half, kk * C : (kk + 1) * C
                ]
    for peer in q_peers:
        send(p2_send.at[peer[0] % 4], p2_recv.at[q], P2, peer)
    p2_recv[q] = p2_send[q]
    arrived(P2, p2_recv.at[pl.ds(0, 3)])
    z2_send[...] = dot(table(4), p2_recv[...].reshape(size, 2 * C)).astype(BF16).reshape(planes, 16, 2 * C)
    for peer in z_peers:
        send(z2_send.at[peer[0] // 4], z2_recv.at[z], Z2, peer)
    z2_recv[z] = z2_send[z]
    arrived(Z2, z2_recv.at[pl.ds(0, planes - 1)])
    filtered = dot(table(5), z2_recv[...].reshape(size, 2 * C)) * row_scale

    square_ones = jnp.ones((C, C), BF16)
    for r in range(2):
        values = mixed[r] + filtered[:, r * C : (r + 1) * C]
        mixed[r] = values
        hi = values.astype(BF16)
        local_mean = dot(hi, square_ones) * (1.0 / C)
        centered = (values - local_mean).astype(BF16)
        y_send[r] = centered
        wide = centered.astype(F32)
        sq_hi, sq_lo = split_hi_lo(wide * wide)
        row_mean = dot_nt(ones, hi)[0:1] * (1.0 / C)
        row_sum = dot_nt(ones, centered)[0:1]
        row_square = (dot_nt(ones, sq_hi) + dot_nt(ones, sq_lo))[0:1]
        st2_send[r] = stack_rows([row_mean, row_sum, row_square], 8, width)
    for g in g_peers:
        send(y_send.at[g // across], y_recv.at[grp], Y, (row, g))
        send(st2_send.at[g // across], st2_recv.at[grp], ST2, (row, g))
    y_recv[grp] = y_send[y_hi]
    st2_recv[grp] = st2_send[y_hi]

    wait_on(recv_sem.at[WUP], peer_up.at[pl.ds(0, up.shape[0] // 2)])
    drains.append((WUP, peer_up.at[pl.ds(0, up.shape[0] // 2)]))
    send(peer_up.at[half_up], peer_up.at[half_up], FUP, sibling)
    wait_on(recv_sem.at[WDN], peer_down.at[pl.ds(0, hidden // 2)])
    drains.append((WDN, peer_down.at[pl.ds(0, hidden // 2)]))
    send(peer_down.at[half_dn], peer_down.at[half_dn], FDN, sibling)

    arrived(ST2, st2_recv.at[pl.ds(0, groups - 1)])
    sent = [st2_recv[g] for g in range(groups)]
    mean = sent[0][0:1] + sent[0][1:2] * (1.0 / C)
    for g in range(1, groups):
        mean = mean + (sent[g][0:1] + sent[g][1:2] * (1.0 / C))
    mean = mean * (1.0 / groups)
    offsets = [sent[g][0:1] - mean for g in range(groups)]
    square = jnp.zeros((1, width), F32)
    for g in range(groups):
        square = square + (sent[g][2:3] + 2.0 * offsets[g] * sent[g][1:2] + float(C) * offsets[g] * offsets[g])
    scale = lax.rsqrt(square / total_channels + epsilon)
    off_hi, off_lo = split_hi_lo(columns_of(offsets, width))
    scale = columns_of([scale], width)[:, 0:1]

    arrived(Y, y_recv.at[pl.ds(0, groups - 1)])
    flat = jnp.concatenate([y_recv[g] for g in range(groups)], axis=1)

    def hidden_of(weights, sums):
        shift = dot(off_hi, sums[0]) + dot(off_lo, sums[0]) + dot(off_hi, sums[1])
        return gelu((dot(flat, weights) + shift) * scale).astype(BF16)

    hid_own[...] = hidden_of(up[...], own_sums)
    arrived(FUP, peer_up.at[pl.ds(0, up.shape[0] // 2)])
    peer_sums = column_sums(peer_up[...])
    hid_peer[...] = hidden_of(peer_up[...], peer_sums)
    arrived(FDN, peer_down.at[pl.ds(0, hidden // 2)])
    pairs = groups // 2
    for i in range(pairs):
        pair = lax.rem(grp // 2 + 1 + i, pairs)
        columns = pl.ds(pl.multiple_of(pair * 2 * C, 2 * C), 2 * C)
        part = dot(hid_own[...], down[:, columns]) + dot(hid_peer[...], peer_down[:, columns])
        rs_send[2 * pair] = part[:, :C].astype(BF16)
        rs_send[2 * pair + 1] = part[:, C:].astype(BF16)
        if i < pairs - 1:
            for g in (2 * pair, 2 * pair + 1):
                send(rs_send.at[g], rs_recv.at[grp], RS, (row, g))
    other = grp + 1 - 2 * (grp % 2)
    send(rs_send.at[other], rs_recv.at[grp], RS, (row, other))
    rs_recv[grp] = rs_send[grp]

    for at, halo in ((HUP, halo_up), (HDN, halo_down), (HLF, halo_left), (HRT, halo_right)):
        arrived(at, halo)
    tile_rows = now.shape[1]
    row_at = lax.broadcasted_iota(jnp.int32, (tile_rows, lanes), 0)
    lane_at = lax.broadcasted_iota(jnp.int32, (tile_rows, lanes), 1)
    own = [now[0], now[1]]
    base = []
    for comp in range(2):
        above = jnp.where(row == 0, 0.0, halo_up[comp, 7:8, :])
        below = jnp.where(row == rows - 1, 0.0, halo_down[comp, 0:1, :])
        left = jnp.where(grp == 0, 0.0, halo_left[comp, :, C - 1 : C])
        right = jnp.where(grp == groups - 1, 0.0, halo_right[comp, :, 0:1])
        center = own[comp]
        up_shift = jnp.where(row_at == tile_rows - 1, below, jnp.roll(center, -1, axis=0))
        down_shift = jnp.where(row_at == 0, above, jnp.roll(center, 1, axis=0))
        from_right = jnp.where(lane_at == lanes - 1, right, jnp.roll(center, -1, axis=1))
        from_left = jnp.where(lane_at == 0, left, jnp.roll(center, 1, axis=1))
        laplace = up_shift + down_shift + from_right + from_left - 4.0 * center
        rotated = own[1] if comp == 0 else -own[0]
        base.append(center + time_step * (coriolis * rotated + viscosity * laplace))

    arrived(RS, rs_recv.at[pl.ds(0, groups - 1)])
    for r in range(2):
        values = rs_recv[r * across].astype(F32)
        for i in range(1, across):
            values = values + rs_recv[r * across + i].astype(F32)
        bo[r] = (mixed[r] + values).astype(BF16)
    tile = width // groups

    def tokens_of(g):
        return bo.at[:, pl.ds(pl.multiple_of(g * tile, tile), tile)]

    for g in g_peers:
        send(tokens_of(g), bo_recv.at[grp], BO, (row, g))
    out_copy = pltpu.make_async_copy(bo, bo_hbm, out_sem.at[0])
    out_copy.start()
    bo_recv[grp] = bo[:, pl.ds(pl.multiple_of(grp * tile, tile), tile)]
    arrived(HW, hw_recv.at[pl.ds(0, groups - 1)])
    arrived(BO, bo_recv.at[pl.ds(0, groups - 1)])
    velocity = jnp.zeros((C, 2 * tile), F32)
    for g in range(0, groups, 2):
        weights = jnp.concatenate([hw_recv[g], hw_recv[g + 1]], axis=1)
        values = jnp.concatenate(
            [bo_recv[g].reshape(2 * tile, C), bo_recv[g + 1].reshape(2 * tile, C)], axis=1
        )
        velocity = velocity + dot_nt(weights, values)

    wide = 2 * lanes
    source = lax.broadcasted_iota(jnp.int32, (2 * tile, wide), 0)
    target = lax.broadcasted_iota(jnp.int32, (2 * tile, wide), 1) // PATCH
    spread = jnp.where(source == target, 1.0, 0.0).astype(BF16)
    vel_hi, vel_lo = split_hi_lo(velocity)
    spread_out = dot(vel_hi, spread) + dot(vel_lo, spread)
    x_row = lax.broadcasted_iota(jnp.int32, (C, wide), 0) % PATCH
    x_lane = lax.broadcasted_iota(jnp.int32, (C, wide), 1) % PATCH
    kept = jnp.where(x_row == x_lane, spread_out, 0.0).reshape(C // PATCH, PATCH, wide)
    cells = jnp.sum(kept, axis=1)
    relative = []
    for comp in range(2):
        part = cells[comp * PATCH : (comp + 1) * PATCH]
        ice_vel = jnp.concatenate([part[:, :lanes], part[:, lanes:]], axis=0)
        relative.append(ice_vel - own[comp])
    speed = jnp.sqrt(relative[0] * relative[0] + relative[1] * relative[1] + speed_floor)
    drag = (time_step * drag_coef) * ice[...].astype(F32) * speed
    open_water = land[...].astype(F32)
    for comp in range(2):
        ocean[comp] = open_water * (base[comp] + drag * relative[comp])
    ocean_copy = pltpu.make_async_copy(ocean, oc_hbm, out_sem.at[1])
    ocean_copy.start()

    for at, like in drains:
        wait_on(send_sem.at[at], like)
    out_copy.wait()
    ocean_copy.wait()


def body(tokens, spec_first, spec_second, up_weight, down_weight, head_weight, ocean_vel, land_mask, ice_mask):
    planes = lax.axis_size("row") // 4
    groups = lax.axis_size("grp")
    _, width, _ = tokens.shape
    embed, hidden = up_weight.shape
    _, tile_rows, lanes = ocean_vel.shape
    size, quarter, tile = 16 * planes, 4 * planes, width // groups
    tables = jnp.asarray(dft_tables(planes))
    args = (
        tokens, spec_first, spec_second, up_weight, down_weight, head_weight, ocean_vel, land_mask, ice_mask, tables,
    )
    copies = [pltpu.VMEM(a.shape, a.dtype) for a in args]
    scratch = copies + [
        pltpu.VMEM((8, width), F32),
        pltpu.VMEM((groups, 8, width), F32),
        pltpu.VMEM((planes, 16, 2 * C), BF16),
        pltpu.VMEM((planes, 16, 2 * C), BF16),
        pltpu.VMEM((4, quarter, 2 * C), BF16),
        pltpu.VMEM((4, quarter, 2 * C), BF16),
        pltpu.VMEM((4, quarter, 2 * C), BF16),
        pltpu.VMEM((4, quarter, 2 * C), BF16),
        pltpu.VMEM((planes, 16, 2 * C), BF16),
        pltpu.VMEM((planes, 16, 2 * C), BF16),
        pltpu.VMEM((2, width, C), F32),
        pltpu.VMEM((2, width, C), BF16),
        pltpu.VMEM((groups, width, C), BF16),
        pltpu.VMEM((2, 8, width), F32),
        pltpu.VMEM((groups, 8, width), F32),
        pltpu.VMEM((embed, hidden), BF16),
        pltpu.VMEM((hidden, embed), BF16),
        pltpu.VMEM((width, hidden), BF16),
        pltpu.VMEM((width, hidden), BF16),
        pltpu.VMEM((groups, width, C), BF16),
        pltpu.VMEM((groups, width, C), BF16),
        pltpu.VMEM((2, width, C), BF16),
        pltpu.VMEM((groups, 2, tile, C), BF16),
        pltpu.VMEM((C, C), BF16),
        pltpu.VMEM((groups, C, C), BF16),
        pltpu.VMEM((2, tile_rows, lanes), F32),
        pltpu.VMEM((2, 8, lanes), F32),
        pltpu.VMEM((2, 8, lanes), F32),
        pltpu.VMEM((2, tile_rows, C), F32),
        pltpu.VMEM((2, tile_rows, C), F32),
        pltpu.VMEM((2, tile_rows, lanes), F32),
        pltpu.SemaphoreType.DMA((len(args),)),
        pltpu.SemaphoreType.DMA((18,)),
        pltpu.SemaphoreType.DMA((18,)),
        pltpu.SemaphoreType.DMA((2,)),
    ]
    return pl.pallas_call(
        functools.partial(kernel, planes, groups),
        out_shape=(
            jax.ShapeDtypeStruct(tokens.shape, BF16),
            jax.ShapeDtypeStruct(ocean_vel.shape, F32),
        ),
        in_specs=[pl.BlockSpec(memory_space=pl.ANY)] * len(args),
        out_specs=[pl.BlockSpec(memory_space=pl.ANY)] * 2,
        scratch_shapes=scratch,
        compiler_params=pltpu.CompilerParams(
            collective_id=0, has_side_effects=True, vmem_limit_bytes=40 * 1024 * 1024
        ),
    )(*args)


def solution(mesh):
    placed = (
        P("row", None, "grp"),
        P(None, "grp", None),
        P(None, "grp", None),
        P(None, "grp"),
        P("grp", None),
        P("grp", None),
        P(None, "row", "grp"),
        P("row", "grp"),
        P("row", "grp"),
    )
    return jax.shard_map(
        body,
        mesh=mesh,
        in_specs=placed,
        out_specs=(P("row", None, "grp"), P(None, "row", "grp")),
        check_vma=False,
    )
```

```python
import functools
import math

import jax
import jax.numpy as jnp
import ml_dtypes
import numpy as np
from jax import lax
from jax.experimental import pallas as pl
from jax.experimental.pallas import tpu as pltpu
from jax.sharding import PartitionSpec as P

PATCH = 8
C = 128

epsilon = 1e-05
shrink_level = 0.01
drag_coef = 0.25
time_step = 0.5
coriolis = 0.3
viscosity = 1.0
speed_floor = 0.01

F32 = jnp.float32
BF16 = jnp.bfloat16
MESH = pl.DeviceIdType.MESH


def dft_tables(rows):
    height, width = 2 * rows, 4 * rows
    d, r, kk, part = (v.reshape(-1, 1) for v in np.meshgrid(range(rows), range(2), range(2), range(2), indexing="ij"))
    k = 2 * d + kk
    r_col, w = (v.reshape(1, -1) for v in np.meshgrid(range(2), range(width), indexing="ij"))
    angle = 2.0 * np.pi * ((k * w) % width) / width
    row_fwd = np.where(r == r_col, np.where(part == 0, np.cos(angle), -np.sin(angle)), 0.0)
    row_bwd = (np.where(k == 0, 1.0, 2.0) * row_fwd).T
    kk_row, part_row, a = (
        v.reshape(-1, 1) for v in np.meshgrid(range(2), range(2), range(height), indexing="ij")
    )
    h, kk, part = (2 * d + r).T, kk.T, part.T
    angle = 2.0 * np.pi * ((a * h) % height) / height
    cos, sin = np.cos(angle), np.sin(angle)
    real = np.where(part == 0, cos, sin)
    imag = np.where(part == 0, -sin, cos)
    col_fwd = np.where(kk_row == kk, np.where(part_row == 0, real, imag), 0.0)
    return np.stack([row_fwd, col_fwd, col_fwd.T, row_bwd]).astype(ml_dtypes.bfloat16)


def dot(a, b):
    return jnp.dot(a, b, preferred_element_type=F32)


def dot_nt(a, b):
    return lax.dot_general(a, b, (((1,), (1,)), ((), ())), preferred_element_type=F32)


def split_hi_lo(values):
    hi = values.astype(BF16)
    return hi, (values - hi.astype(F32)).astype(BF16)


def soft_shrink(values):
    return values - jnp.clip(values, -shrink_level, shrink_level)


def gelu(values):
    return 0.5 * values * (1.0 + lax.erf(values * (1.0 / math.sqrt(2.0))))


def far_first(count):
    return sorted(range(1, count), key=lambda i: -min(i, count - i))


def complex_matrix(ref):
    real, imag = ref[0], ref[1]
    top = jnp.concatenate([real, imag], axis=1)
    low = jnp.concatenate([-imag, real], axis=1)
    return jnp.concatenate([top, low], axis=0)


def stack_rows(rows, count, width):
    at = lax.broadcasted_iota(jnp.int32, (count, width), 0)
    out = jnp.zeros((count, width), F32)
    for i, values in enumerate(rows):
        out = jnp.where(at == i, values, out)
    return out


def stack_halves(rows, width):
    half = width // 2
    return stack_rows([part for values in rows for part in (values[:, :half], values[:, half:])], 8, half)


def whole_row(values, i):
    return jnp.concatenate([values[2 * i : 2 * i + 1], values[2 * i + 1 : 2 * i + 2]], axis=1)


def columns_of(rows, width):
    top = stack_rows(rows, 8, width)
    return jnp.concatenate([top, jnp.zeros((C - 8, width), F32)], axis=0).T


def kernel(
    rows,
    groups,
    tok_hbm, first_hbm, second_hbm, up_hbm, down_hbm, head_hbm, vel_hbm, land_hbm, ice_hbm, tab_hbm,
    bo_hbm, oc_hbm,
    tok, first, second, up, down, head, vel, land, ice, tab,
    st1_send, st1_recv, z1_send, z1_recv, z2_send, z2_recv,
    mixed, y_send, y_recv, st2_send, st2_recv, peer_up, peer_down, rs_send, rs_recv,
    bo, vf_send, vf_recv, hw_recv, now, halo_up, halo_down, halo_left, halo_right, ocean,
    local_sem, send_sem, recv_sem, out_sem,
):
    width = tok.shape[1]
    total_channels = C * groups
    row, grp = lax.axis_index("row"), lax.axis_index("grp")
    core, side = row % 2, grp % 2
    hidden = up.shape[1]

    r_peers = [lax.rem(row + i, rows) for i in far_first(rows)]
    g_peers = [lax.rem(grp + i, groups) for i in far_first(groups)]
    row_above, row_below = lax.rem(row + rows - 1, rows), lax.rem(row + 1, rows)
    weight_peer = (row, grp + 1 - 2 * side)
    sibling = (row + 1 - 2 * core, grp)
    greeted = [(r, grp) for r in r_peers] + [(row, g) for g in g_peers]
    barrier = pltpu.get_barrier_semaphore()
    for peer in greeted:
        pl.semaphore_signal(barrier, inc=1, device_id=peer, device_id_type=MESH)

    loads = {}
    for i, (name, src, dst) in enumerate(
        [
            ("tok", tok_hbm, tok),
            ("vel", vel_hbm, vel),
            ("land", land_hbm, land),
            ("head", head_hbm, head),
            ("tab0", tab_hbm.at[0], tab.at[0]),
            ("first", first_hbm, first),
            ("second", second_hbm, second),
            ("tab1", tab_hbm.at[1], tab.at[1]),
            ("tab2", tab_hbm.at[2], tab.at[2]),
            ("tab3", tab_hbm.at[3], tab.at[3]),
            ("up", up_hbm, up),
            ("down", down_hbm, down),
            ("ice", ice_hbm, ice),
        ]
    ):
        loads[name] = pltpu.make_async_copy(src, dst, local_sem.at[i])
        loads[name].start()

    ones = jnp.ones((16, C), BF16)
    loads["tok"].wait()
    sums = []
    squares = []
    for r in range(2):
        values = tok[r]
        wide = values.astype(F32)
        hi, lo = split_hi_lo(wide * wide)
        sums.append(dot_nt(ones, values)[0:1])
        squares.append((dot_nt(ones, hi) + dot_nt(ones, lo))[0:1])
    st1_send[...] = stack_halves(sums + squares, width)
    st1_recv[grp] = st1_send[...]
    loads["head"].wait()
    hw_recv[grp] = head[...]
    loads["vel"].wait()
    loads["land"].wait()
    open_water = land[...].astype(F32)
    now[0] = vel[0] * open_water
    now[1] = vel[1] * open_water

    pl.semaphore_wait(barrier, len(greeted))

    drains = []

    def send(src, dst, at, peer):
        pltpu.make_async_remote_copy(
            src_ref=src,
            dst_ref=dst,
            send_sem=send_sem.at[at],
            recv_sem=recv_sem.at[at],
            device_id=peer,
            device_id_type=MESH,
        ).start()

    def wait_on(sem, like):
        pltpu.make_async_copy(like, like, sem).wait()

    def arrived(at, like):
        wait_on(recv_sem.at[at], like)
        drains.append((at, like))

    ST1, WUP, WDN, HW, HUP, HDN, HLF, HRT, ST2, FUP, FDN, RS, VF = range(13)
    Z1, Z2, Y = 13, 14, (15, 16)

    for g in g_peers:
        send(st1_send, st1_recv.at[grp], ST1, (row, g))
    half_up = pl.ds(pl.multiple_of(core * (up.shape[0] // 2), up.shape[0] // 2), up.shape[0] // 2)
    half_dn = pl.ds(pl.multiple_of(core * (hidden // 2), hidden // 2), hidden // 2)
    send(up_hbm.at[half_up], peer_up.at[half_up], WUP, weight_peer)
    send(down_hbm.at[half_dn], peer_down.at[half_dn], WDN, weight_peer)

    arrived(ST1, st1_recv.at[pl.ds(0, groups - 1)])
    totals = st1_recv[0]
    for g in range(1, groups):
        totals = totals + st1_recv[g]
    totals = totals / total_channels
    mean = [whole_row(totals, r) for r in range(2)]
    scale = [lax.rsqrt(whole_row(totals, 2 + r) - mean[r] * mean[r] + epsilon) for r in range(2)]
    stats = columns_of(mean + scale, width)
    loads["tab0"].wait()
    normed = []
    for r in range(2):
        inputs = tok[r].astype(F32)
        normed.append((inputs - stats[:, r : r + 1]) * stats[:, 2 + r : 3 + r])
        mixed[r] = inputs + normed[r]

    height, size = 2 * rows, 8 * rows
    row_scale, col_scale = 1.0 / math.sqrt(width), 1.0 / math.sqrt(height)
    flat = jnp.concatenate([normed[0].astype(BF16), normed[1].astype(BF16)], axis=0)
    z1_send[...] = (dot(tab[0], flat) * row_scale).reshape(rows, 8, C).astype(BF16)
    for r in r_peers:
        send(z1_send.at[r], z1_recv.at[row], Z1, (r, grp))
    z1_recv[row] = z1_send[row]

    for g in g_peers:
        send(head, hw_recv.at[grp], HW, (row, g))
    send(now.at[:, pl.ds(8, 8)], halo_up, HUP, (row_below, grp))
    send(now.at[:, pl.ds(0, 8)], halo_down, HDN, (row_above, grp))
    lanes = now.shape[2]
    send(now.at[:, :, pl.ds(lanes - C, C)], halo_left, HLF, (row, lax.rem(grp + 1, groups)))
    send(now.at[:, :, pl.ds(0, C)], halo_right, HRT, (row, lax.rem(grp + groups - 1, groups)))
    loads["first"].wait()
    loads["second"].wait()
    weight_one = complex_matrix(first).astype(BF16)
    weight_two, weight_two_lo = split_hi_lo(complex_matrix(second))
    loads["up"].wait()
    loads["down"].wait()
    loads["ice"].wait()
    for i in range(1, 4):
        loads["tab" + str(i)].wait()
    block_at = lax.broadcasted_iota(jnp.int32, (16, total_channels), 0)
    block_of = lax.broadcasted_iota(jnp.int32, (16, total_channels), 1) // C
    pick = jnp.where(block_at == block_of, 1.0, 0.0).astype(BF16)

    def column_sums(weights):
        sums = dot(pick, weights)
        hi, lo = split_hi_lo(sums)
        pad = jnp.zeros((C - 16, weights.shape[1]), BF16)
        return jnp.concatenate([hi, pad], axis=0), jnp.concatenate([lo, pad], axis=0)

    def through(columns, sums):
        return dot(columns[0], sums[0]) + dot(columns[1], sums[0]) + dot(columns[0], sums[1])

    own_sums = column_sums(up[...])

    def blocks(values):
        return [values[i * height : (i + 1) * height] for i in range(4)]

    arrived(Z1, z1_recv.at[pl.ds(0, rows - 1)])
    columns = z1_recv[...].astype(F32).reshape(size, C).astype(BF16)
    freq = blocks((dot(tab[1], columns) * col_scale).astype(BF16))
    freq = jnp.concatenate(
        [jnp.concatenate(freq[:2], axis=1), jnp.concatenate(freq[2:], axis=1)], axis=0
    )
    hid = jax.nn.relu(dot(freq, weight_one)).astype(BF16)
    mix = soft_shrink(dot(hid, weight_two) + dot(hid, weight_two_lo)).astype(BF16)
    mix = jnp.concatenate(
        [mix[kk * height : (kk + 1) * height, p * C : (p + 1) * C] for kk in range(2) for p in range(2)], axis=0
    )
    z2_send[...] = (dot(tab[2], mix) * col_scale).reshape(rows, 8, C).astype(BF16)
    for r in r_peers:
        send(z2_send.at[r], z2_recv.at[row], Z2, (r, grp))
    z2_recv[row] = z2_send[row]

    arrived(Z2, z2_recv.at[pl.ds(0, rows - 1)])
    columns = z2_recv[...].astype(F32).reshape(size, C).astype(BF16)
    square_ones = jnp.ones((C, C), BF16)
    for r in range(2):
        values = mixed[r] + dot(tab[3, r * width : (r + 1) * width], columns) * row_scale
        mixed[r] = values
        hi = values.astype(BF16)
        local_mean = dot(hi, square_ones) * (1.0 / C)
        centered = (values - local_mean).astype(BF16)
        y_send[r] = centered
        wide = centered.astype(F32)
        sq_hi, sq_lo = split_hi_lo(wide * wide)
        row_mean = dot_nt(ones, hi)[0:1] * (1.0 / C)
        row_sum = dot_nt(ones, centered)[0:1]
        row_square = (dot_nt(ones, sq_hi) + dot_nt(ones, sq_lo))[0:1]
        st2_send[r] = stack_halves([row_mean, row_sum, row_square], width)
    for g in g_peers:
        send(st2_send.at[g % 2], st2_recv.at[grp], ST2, (row, g))
    part = width // 2
    for t in range(2):
        for g in g_peers:
            send(y_send.at[g % 2, pl.ds(t * part, part)], y_recv.at[t, grp], Y[t], (row, g))
        y_recv[t, grp] = y_send[side, t * part : (t + 1) * part]
    st2_recv[grp] = st2_send[side]

    tile = width // groups

    wait_on(recv_sem.at[WUP], peer_up.at[pl.ds(0, up.shape[0] // 2)])
    drains.append((WUP, peer_up.at[pl.ds(0, up.shape[0] // 2)]))
    send(peer_up.at[half_up], peer_up.at[half_up], FUP, sibling)
    wait_on(recv_sem.at[WDN], peer_down.at[pl.ds(0, hidden // 2)])
    drains.append((WDN, peer_down.at[pl.ds(0, hidden // 2)]))
    send(peer_down.at[half_dn], peer_down.at[half_dn], FDN, sibling)

    arrived(HW, hw_recv.at[pl.ds(0, groups - 1)])
    whole_head = hw_recv[...].reshape(total_channels, C)
    head_sums = column_sums(whole_head)
    own_head = dot(down[...], whole_head).astype(BF16)
    arrived(FUP, peer_up.at[pl.ds(0, up.shape[0] // 2)])
    peer_sums = column_sums(peer_up[...])
    arrived(FDN, peer_down.at[pl.ds(0, hidden // 2)])
    peer_head = dot(peer_down[...], whole_head).astype(BF16)
    arrived(ST2, st2_recv.at[pl.ds(0, groups - 1)])
    sent = [[whole_row(st2_recv[g], i) for i in range(3)] for g in range(groups)]
    mean = jnp.zeros((1, width), F32)
    for row_mean, row_sum, _ in sent:
        mean = mean + (row_mean + row_sum * (1.0 / C))
    mean = mean * (1.0 / groups)
    offsets = [row_mean - mean for row_mean, _, _ in sent]
    square = jnp.zeros((1, width), F32)
    for offset, (_, row_sum, row_square) in zip(offsets, sent):
        square = square + (row_square + 2.0 * offset * row_sum + float(C) * offset * offset)
    scale = lax.rsqrt(square / total_channels + epsilon)
    local_means = split_hi_lo(columns_of([row_mean for row_mean, _, _ in sent], width))
    offsets = split_hi_lo(columns_of(offsets, width))
    scale = columns_of([scale], width)[:, 0:1]

    other = weight_peer[1]
    pairs = groups // 2
    for t in range(2):
        arrived(Y[t], y_recv.at[t, pl.ds(0, groups - 1)])
        flat = jnp.concatenate([y_recv[t, g] for g in range(groups)], axis=1)
        rows_at = slice(t * part, (t + 1) * part)

        def hidden_of(weights, sums):
            shift = through([part_of[rows_at] for part_of in offsets], sums)
            return gelu((dot(flat, weights) + shift) * scale[rows_at]).astype(BF16)

        hid_own = hidden_of(up[...], own_sums)
        hid_peer = hidden_of(peer_up[...], peer_sums)

        velocity = dot(hid_own, own_head) + dot(hid_peer, peer_head)
        before = dot(flat, whole_head) + through([part_of[rows_at] for part_of in local_means], head_sums)
        tiles = range(t * (groups // 2), (t + 1) * (groups // 2))
        for i, g in enumerate(tiles):
            tokens_at = slice(i * tile, (i + 1) * tile)
            mine = jnp.where(grp // 2 == g // 2, 1.0, 0.0)
            vf_send[g] = (velocity[tokens_at] + mine * before[tokens_at]).astype(BF16)
        for g in tiles:

            @pl.when(grp != g)
            def _():
                send(vf_send.at[g], vf_recv.at[grp], VF, (row, g))

        for i in range(pairs):
            pair = lax.rem(grp // 2 + 1 + i, pairs)
            columns = pl.ds(pl.multiple_of(pair * 2 * C, 2 * C), 2 * C)
            partial = dot(hid_own, down[:, columns]) + dot(hid_peer, peer_down[:, columns])
            partial = partial.astype(BF16)
            rs_send[2 * pair, rows_at] = partial[:, :C]
            rs_send[2 * pair + 1, rows_at] = partial[:, C:]
            if i < pairs - 1:
                for g in (2 * pair, 2 * pair + 1):
                    send(rs_send.at[g, pl.ds(t * part, part)], rs_recv.at[grp, pl.ds(t * part, part)], RS, (row, g))
        send(rs_send.at[other, pl.ds(t * part, part)], rs_recv.at[grp, pl.ds(t * part, part)], RS, (row, other))
    vf_recv[grp] = vf_send[grp]
    rs_recv[grp] = rs_send[grp]

    for at, halo in ((HUP, halo_up), (HDN, halo_down), (HLF, halo_left), (HRT, halo_right)):
        arrived(at, halo)
    tile_rows = now.shape[1]
    row_at = lax.broadcasted_iota(jnp.int32, (tile_rows, lanes), 0)
    lane_at = lax.broadcasted_iota(jnp.int32, (tile_rows, lanes), 1)
    own = [now[0], now[1]]
    base = []
    for comp in range(2):
        above = jnp.where(row == 0, 0.0, halo_up[comp, 7:8, :])
        below = jnp.where(row == rows - 1, 0.0, halo_down[comp, 0:1, :])
        left = jnp.where(grp == 0, 0.0, halo_left[comp, :, C - 1 : C])
        right = jnp.where(grp == groups - 1, 0.0, halo_right[comp, :, 0:1])
        center = own[comp]
        up_shift = jnp.where(row_at == tile_rows - 1, below, jnp.roll(center, -1, axis=0))
        down_shift = jnp.where(row_at == 0, above, jnp.roll(center, 1, axis=0))
        from_right = jnp.where(lane_at == lanes - 1, right, jnp.roll(center, -1, axis=1))
        from_left = jnp.where(lane_at == 0, left, jnp.roll(center, 1, axis=1))
        laplace = up_shift + down_shift + from_right + from_left - 4.0 * center
        rotated = own[1] if comp == 0 else -own[0]
        base.append(center + time_step * (coriolis * rotated + viscosity * laplace))

    arrived(VF, vf_recv.at[pl.ds(0, groups - 1)])
    velocity = []
    for r in range(2):
        values = jnp.zeros((tile, C), F32)
        for g in range(r, groups, 2):
            values = values + vf_recv[g].astype(F32)
        velocity.append(values)
    velocity.append(jnp.zeros((C - 2 * tile, C), F32))
    velocity = jnp.concatenate(velocity, axis=0).T

    wide = 2 * lanes
    source = lax.broadcasted_iota(jnp.int32, (C, wide), 0)
    target = lax.broadcasted_iota(jnp.int32, (C, wide), 1) // PATCH
    spread = jnp.where(source == target, 1.0, 0.0).astype(BF16)
    vel_hi, vel_lo = split_hi_lo(velocity)
    spread_out = dot(vel_hi, spread) + dot(vel_lo, spread)
    x_row = lax.broadcasted_iota(jnp.int32, (C, wide), 0) % PATCH
    x_lane = lax.broadcasted_iota(jnp.int32, (C, wide), 1) % PATCH
    kept = jnp.where(x_row == x_lane, spread_out, 0.0).reshape(C // PATCH, PATCH, wide)
    cells = jnp.sum(kept, axis=1)
    relative = []
    for comp in range(2):
        part = cells[comp * PATCH : (comp + 1) * PATCH]
        ice_vel = jnp.concatenate([part[:, :lanes], part[:, lanes:]], axis=0)
        relative.append(ice_vel - own[comp])
    speed = jnp.sqrt(relative[0] * relative[0] + relative[1] * relative[1] + speed_floor)
    drag = (time_step * drag_coef) * ice[...].astype(F32) * speed
    open_water = land[...].astype(F32)
    for comp in range(2):
        ocean[comp] = open_water * (base[comp] + drag * relative[comp])
    ocean_copy = pltpu.make_async_copy(ocean, oc_hbm, out_sem.at[1])
    ocean_copy.start()

    arrived(RS, rs_recv.at[pl.ds(0, groups - 1)])
    for r in range(2):
        values = rs_recv[r].astype(F32)
        for g in range(r + 2, groups, 2):
            values = values + rs_recv[g].astype(F32)
        bo[r] = (mixed[r] + values).astype(BF16)
    out_copy = pltpu.make_async_copy(bo, bo_hbm, out_sem.at[0])
    out_copy.start()

    for at, like in drains:
        wait_on(send_sem.at[at], like)
    out_copy.wait()
    ocean_copy.wait()


def copy_kernel(bo_in, oc_in, bo_out, oc_out, bo, oc, sem):
    loads = [pltpu.make_async_copy(bo_in, bo, sem.at[0]), pltpu.make_async_copy(oc_in, oc, sem.at[1])]
    stores = [pltpu.make_async_copy(bo, bo_out, sem.at[2]), pltpu.make_async_copy(oc, oc_out, sem.at[3])]
    for load in loads:
        load.start()
    for load, store in zip(loads, stores):
        load.wait()
        store.start()
    for store in stores:
        store.wait()


def body(tokens, spec_first, spec_second, up_weight, down_weight, head_weight, ocean_vel, land_mask, ice_mask):
    rows = lax.axis_size("row")
    groups = lax.axis_size("grp")
    _, width, _ = tokens.shape
    embed, hidden = up_weight.shape
    _, tile_rows, lanes = ocean_vel.shape
    tile = width // groups
    tables = jnp.asarray(dft_tables(rows))
    args = (
        tokens, spec_first, spec_second, up_weight, down_weight, head_weight, ocean_vel, land_mask, ice_mask, tables,
    )
    copies = [pltpu.VMEM(a.shape, a.dtype) for a in args]
    scratch = copies + [
        pltpu.VMEM((8, width // 2), F32),
        pltpu.VMEM((groups, 8, width // 2), F32),
        pltpu.VMEM((rows, 8, C), BF16),
        pltpu.VMEM((rows, 8, C), BF16),
        pltpu.VMEM((rows, 8, C), BF16),
        pltpu.VMEM((rows, 8, C), BF16),
        pltpu.VMEM((2, width, C), F32),
        pltpu.VMEM((2, width, C), BF16),
        pltpu.VMEM((2, groups, width // 2, C), BF16),
        pltpu.VMEM((2, 8, width // 2), F32),
        pltpu.VMEM((groups, 8, width // 2), F32),
        pltpu.VMEM((embed, hidden), BF16),
        pltpu.VMEM((hidden, embed), BF16),
        pltpu.VMEM((groups, width, C), BF16),
        pltpu.VMEM((groups, width, C), BF16),
        pltpu.VMEM((2, width, C), BF16),
        pltpu.VMEM((groups, tile, C), BF16),
        pltpu.VMEM((groups, tile, C), BF16),
        pltpu.VMEM((groups, C, C), BF16),
        pltpu.VMEM((2, tile_rows, lanes), F32),
        pltpu.VMEM((2, 8, lanes), F32),
        pltpu.VMEM((2, 8, lanes), F32),
        pltpu.VMEM((2, tile_rows, C), F32),
        pltpu.VMEM((2, tile_rows, C), F32),
        pltpu.VMEM((2, tile_rows, lanes), F32),
        pltpu.SemaphoreType.DMA((len(args) + 3,)),
        pltpu.SemaphoreType.DMA((17,)),
        pltpu.SemaphoreType.DMA((17,)),
        pltpu.SemaphoreType.DMA((2,)),
    ]
    outs = (
        jax.ShapeDtypeStruct(tokens.shape, BF16),
        jax.ShapeDtypeStruct(ocean_vel.shape, F32),
    )
    results = pl.pallas_call(
        functools.partial(kernel, rows, groups),
        out_shape=outs,
        in_specs=[pl.BlockSpec(memory_space=pl.ANY)] * len(args),
        out_specs=[pl.BlockSpec(memory_space=pl.ANY)] * 2,
        scratch_shapes=scratch,
        compiler_params=pltpu.CompilerParams(
            collective_id=0, has_side_effects=True, vmem_limit_bytes=60 * 1024 * 1024
        ),
    )(*args)
    return pl.pallas_call(
        copy_kernel,
        out_shape=outs,
        in_specs=[pl.BlockSpec(memory_space=pl.ANY)] * 2,
        out_specs=[pl.BlockSpec(memory_space=pl.ANY)] * 2,
        scratch_shapes=[pltpu.VMEM(out.shape, out.dtype) for out in outs] + [pltpu.SemaphoreType.DMA((4,))],
    )(*results)


def solution(mesh):
    placed = (
        P("row", None, "grp"),
        P(None, "grp", None),
        P(None, "grp", None),
        P(None, "grp"),
        P("grp", None),
        P("grp", None),
        P(None, "row", "grp"),
        P("row", "grp"),
        P("row", "grp"),
    )
    return jax.shard_map(
        body,
        mesh=mesh,
        in_specs=placed,
        out_specs=(P("row", None, "grp"), P(None, "row", "grp")),
        check_vma=False,
    )
```

```python
import functools
import math

import jax
import jax.numpy as jnp
import ml_dtypes
import numpy as np
from jax import lax
from jax.experimental import pallas as pl
from jax.experimental.pallas import tpu as pltpu
from jax.sharding import PartitionSpec as P

PATCH = 8
C = 128

epsilon = 1e-05
shrink_level = 0.01
drag_coef = 0.25
time_step = 0.5
coriolis = 0.3
viscosity = 1.0
speed_floor = 0.01

F32 = jnp.float32
BF16 = jnp.bfloat16
MESH = pl.DeviceIdType.MESH


def dft_tables(rows):
    height, width = 2 * rows, 4 * rows
    d, r, kk, part = (v.reshape(-1, 1) for v in np.meshgrid(range(rows), range(2), range(2), range(2), indexing="ij"))
    k = 2 * d + kk
    r_col, w = (v.reshape(1, -1) for v in np.meshgrid(range(2), range(width), indexing="ij"))
    angle = 2.0 * np.pi * ((k * w) % width) / width
    row_fwd = np.where(r == r_col, np.where(part == 0, np.cos(angle), -np.sin(angle)), 0.0)
    row_bwd = (np.where(k == 0, 1.0, 2.0) * row_fwd).T
    kk_row, part_row, a = (
        v.reshape(-1, 1) for v in np.meshgrid(range(2), range(2), range(height), indexing="ij")
    )
    h, kk, part = (2 * d + r).T, kk.T, part.T
    angle = 2.0 * np.pi * ((a * h) % height) / height
    cos, sin = np.cos(angle), np.sin(angle)
    real = np.where(part == 0, cos, sin)
    imag = np.where(part == 0, -sin, cos)
    col_fwd = np.where(kk_row == kk, np.where(part_row == 0, real, imag), 0.0)
    return np.stack([row_fwd, col_fwd, col_fwd.T, row_bwd]).astype(ml_dtypes.bfloat16)


def dot(a, b):
    return jnp.dot(a, b, preferred_element_type=F32)


def dot_nt(a, b):
    return lax.dot_general(a, b, (((1,), (1,)), ((), ())), preferred_element_type=F32)


def split_hi_lo(values):
    hi = values.astype(BF16)
    return hi, (values - hi.astype(F32)).astype(BF16)


def soft_shrink(values):
    return values - jnp.clip(values, -shrink_level, shrink_level)


def gelu(values):
    return 0.5 * values * (1.0 + lax.erf(values * (1.0 / math.sqrt(2.0))))


def far_first(count):
    return sorted(range(1, count), key=lambda i: -min(i, count - i))


def complex_matrix(ref):
    real, imag = ref[0], ref[1]
    top = jnp.concatenate([real, imag], axis=1)
    low = jnp.concatenate([-imag, real], axis=1)
    return jnp.concatenate([top, low], axis=0)


def stack_rows(rows, count, width):
    at = lax.broadcasted_iota(jnp.int32, (count, width), 0)
    out = jnp.zeros((count, width), F32)
    for i, values in enumerate(rows):
        out = jnp.where(at == i, values, out)
    return out


def stack_halves(rows, width):
    half = width // 2
    return stack_rows([part for values in rows for part in (values[:, :half], values[:, half:])], 8, half)


def whole_row(values, i):
    return jnp.concatenate([values[2 * i : 2 * i + 1], values[2 * i + 1 : 2 * i + 2]], axis=1)


def columns_of(rows, width):
    top = stack_rows(rows, 8, width)
    return jnp.concatenate([top, jnp.zeros((C - 8, width), F32)], axis=0).T


def kernel(
    rows,
    groups,
    tok_hbm, first_hbm, second_hbm, up_hbm, down_hbm, head_hbm, vel_hbm, land_hbm, ice_hbm, tab_hbm,
    bo_hbm, oc_hbm,
    tok, first, second, up, down, head, vel, land, ice, tab,
    st1_send, st1_recv, z1_send, z1_recv, z2_send, z2_recv,
    mixed, y_send, y_recv, st2_send, st2_recv, peer_up, peer_down, rs_send, rs_recv,
    bo, means, vm_send, vm_recv, vf_send, vf_recv, hw_recv, now, halo_up, halo_down, halo_left, halo_right, ocean,
    local_sem, send_sem, recv_sem, out_sem,
):
    width = tok.shape[1]
    total_channels = C * groups
    row, grp = lax.axis_index("row"), lax.axis_index("grp")
    core, side = row % 2, grp % 2
    hidden = up.shape[1]

    tok_load = pltpu.make_async_copy(tok_hbm, tok, local_sem.at[0])
    tok_load.start()
    weight_peer = (row, grp + 1 - 2 * side)
    sibling = (row + 1 - 2 * core, grp)
    r_peers = [lax.rem(row + i, rows) for i in far_first(rows)]
    planes = rows // 4
    z, y_lo = row // 4, (row // 2) % 2
    far_planes = [lax.rem(z + i, planes) * 4 for i in far_first(planes)]
    staged_peers = []
    for to_core in range(2):
        staged_peers += [z_at + 2 * y_at + to_core for z_at in far_planes for y_at in range(2)]
        staged_peers.append(z * 4 + 2 * (1 - y_lo) + to_core)
    staged_peers.append(sibling[0])
    g_peers = [lax.rem(grp + i, groups) for i in far_first(groups)]
    row_above, row_below = lax.rem(row + rows - 1, rows), lax.rem(row + 1, rows)
    greeted = [(r, grp) for r in r_peers] + [(row, g) for g in g_peers]
    barrier = pltpu.get_barrier_semaphore()
    for peer in greeted:
        pl.semaphore_signal(barrier, inc=1, device_id=peer, device_id_type=MESH)

    loads = {"tok": tok_load}
    for i, (name, src, dst) in enumerate(
        [
            ("vel", vel_hbm, vel),
            ("land", land_hbm, land),
            ("head", head_hbm, head),
            ("tab0", tab_hbm.at[0], tab.at[0]),
            ("first", first_hbm, first),
            ("second", second_hbm, second),
            ("tab1", tab_hbm.at[1], tab.at[1]),
            ("tab2", tab_hbm.at[2], tab.at[2]),
            ("tab3", tab_hbm.at[3], tab.at[3]),
            ("up", up_hbm, up),
            ("down", down_hbm, down),
            ("ice", ice_hbm, ice),
        ]
    ):
        loads[name] = pltpu.make_async_copy(src, dst, local_sem.at[i + 1])
        loads[name].start()

    ones = jnp.ones((16, C), BF16)
    loads["tok"].wait()
    sums = []
    squares = []
    for r in range(2):
        values = tok[r]
        wide = values.astype(F32)
        hi, lo = split_hi_lo(wide * wide)
        sums.append(dot_nt(ones, values)[0:1])
        squares.append((dot_nt(ones, hi) + dot_nt(ones, lo))[0:1])
    st1_send[...] = stack_halves(sums + squares, width)
    st1_recv[grp] = st1_send[...]
    loads["head"].wait()
    hw_recv[grp] = head[...]
    loads["vel"].wait()
    loads["land"].wait()
    open_water = land[...].astype(F32)
    now[0] = vel[0] * open_water
    now[1] = vel[1] * open_water

    pl.semaphore_wait(barrier, len(greeted))

    drains = []

    def send(src, dst, at, peer):
        pltpu.make_async_remote_copy(
            src_ref=src,
            dst_ref=dst,
            send_sem=send_sem.at[at],
            recv_sem=recv_sem.at[at],
            device_id=peer,
            device_id_type=MESH,
        ).start()

    def wait_on(sem, like):
        pltpu.make_async_copy(like, like, sem).wait()

    def arrived(at, like):
        wait_on(recv_sem.at[at], like)
        drains.append((at, like))

    ST1, WUP, WDN, HW, HUP, HDN, HLF, HRT, ST2, FUP, FDN, RS, VF, VM = range(14)
    Z1, Z2, Y = 14, 15, (16, 17, 18)

    for g in g_peers:
        send(st1_send, st1_recv.at[grp], ST1, (row, g))
    half_up = pl.ds(pl.multiple_of(core * (up.shape[0] // 2), up.shape[0] // 2), up.shape[0] // 2)
    half_dn = pl.ds(pl.multiple_of(core * (hidden // 2), hidden // 2), hidden // 2)
    send(up_hbm.at[half_up], peer_up.at[half_up], WUP, weight_peer)
    send(down_hbm.at[half_dn], peer_down.at[half_dn], WDN, weight_peer)

    arrived(ST1, st1_recv.at[pl.ds(0, groups - 1)])
    totals = st1_recv[0]
    for g in range(1, groups):
        totals = totals + st1_recv[g]
    totals = totals / total_channels
    mean = [whole_row(totals, r) for r in range(2)]
    scale = [lax.rsqrt(whole_row(totals, 2 + r) - mean[r] * mean[r] + epsilon) for r in range(2)]
    stats = columns_of(mean + scale, width)
    loads["tab0"].wait()
    normed = []
    for r in range(2):
        inputs = tok[r].astype(F32)
        normed.append((inputs - stats[:, r : r + 1]) * stats[:, 2 + r : 3 + r])
        mixed[r] = inputs + normed[r]

    height, size = 2 * rows, 8 * rows
    row_scale, col_scale = 1.0 / math.sqrt(width), 1.0 / math.sqrt(height)
    flat = jnp.concatenate([normed[0].astype(BF16), normed[1].astype(BF16)], axis=0)
    z1_send[...] = (dot(tab[0], flat) * row_scale).reshape(rows, 8, C).astype(BF16)
    for r in staged_peers:
        send(z1_send.at[r], z1_recv.at[row], Z1, (r, grp))
    z1_recv[row] = z1_send[row]

    for g in g_peers:
        send(head, hw_recv.at[grp], HW, (row, g))
    send(now.at[:, pl.ds(8, 8)], halo_up, HUP, (row_below, grp))
    send(now.at[:, pl.ds(0, 8)], halo_down, HDN, (row_above, grp))
    lanes = now.shape[2]
    send(now.at[:, :, pl.ds(lanes - C, C)], halo_left, HLF, (row, lax.rem(grp + 1, groups)))
    send(now.at[:, :, pl.ds(0, C)], halo_right, HRT, (row, lax.rem(grp + groups - 1, groups)))
    loads["first"].wait()
    loads["second"].wait()
    weight_one = complex_matrix(first).astype(BF16)
    weight_two, weight_two_lo = split_hi_lo(complex_matrix(second))
    loads["up"].wait()
    loads["down"].wait()
    loads["ice"].wait()
    for i in range(1, 4):
        loads["tab" + str(i)].wait()
    block_at = lax.broadcasted_iota(jnp.int32, (16, total_channels), 0) % 8
    block_of = lax.broadcasted_iota(jnp.int32, (16, total_channels), 1) // C
    pick = jnp.where(block_at == block_of, 1.0, 0.0).astype(BF16)

    def column_sums(weights):
        hi, lo = split_hi_lo(dot(pick, weights))
        return jnp.concatenate([hi[:16], lo, jnp.zeros((C - 32, weights.shape[1]), BF16)], axis=0)

    own_sums = column_sums(up[...])

    def blocks(values):
        return [values[i * height : (i + 1) * height] for i in range(4)]

    arrived(Z1, z1_recv.at[pl.ds(0, rows - 1)])
    columns = z1_recv[...].astype(F32).reshape(size, C).astype(BF16)
    freq = blocks((dot(tab[1], columns) * col_scale).astype(BF16))
    freq = jnp.concatenate(
        [jnp.concatenate(freq[:2], axis=1), jnp.concatenate(freq[2:], axis=1)], axis=0
    )
    hid = jax.nn.relu(dot(freq, weight_one)).astype(BF16)
    mix = soft_shrink(dot(hid, weight_two) + dot(hid, weight_two_lo)).astype(BF16)
    mix = jnp.concatenate(
        [mix[kk * height : (kk + 1) * height, p * C : (p + 1) * C] for kk in range(2) for p in range(2)], axis=0
    )
    z2_send[...] = (dot(tab[2], mix) * col_scale).reshape(rows, 8, C).astype(BF16)
    for r in r_peers:
        send(z2_send.at[r], z2_recv.at[row], Z2, (r, grp))
    z2_recv[row] = z2_send[row]

    arrived(Z2, z2_recv.at[pl.ds(0, rows - 1)])
    columns = z2_recv[...].astype(F32).reshape(size, C).astype(BF16)
    square_ones = jnp.ones((C, C), BF16)
    for r in range(2):
        values = mixed[r] + dot(tab[3, r * width : (r + 1) * width], columns) * row_scale
        mixed[r] = values
        hi = values.astype(BF16)
        local_mean = dot(hi, square_ones) * (1.0 / C)
        centered = (values - local_mean).astype(BF16)
        y_send[r] = centered
        wide = centered.astype(F32)
        sq_hi, sq_lo = split_hi_lo(wide * wide)
        row_mean = dot_nt(ones, hi)[0:1] * (1.0 / C)
        row_sum = dot_nt(ones, centered)[0:1]
        row_square = (dot_nt(ones, sq_hi) + dot_nt(ones, sq_lo))[0:1]
        st2_send[r] = stack_halves([row_mean, row_sum, row_square], width)
    for g in g_peers:
        send(st2_send.at[g % 2], st2_recv.at[grp], ST2, (row, g))
    tile = width // groups
    cuts = (0, 2, 5, 8) if groups == 8 else (0, groups // 2, groups)
    parts = range(len(cuts) - 1)
    for t in parts:
        tokens_at = pl.ds(cuts[t] * tile, (cuts[t + 1] - cuts[t]) * tile)
        for g in g_peers:
            send(y_send.at[g % 2, tokens_at], y_recv.at[grp, tokens_at], Y[t], (row, g))
    y_recv[grp] = y_send[side]
    st2_recv[grp] = st2_send[side]

    wait_on(recv_sem.at[WUP], peer_up.at[pl.ds(0, up.shape[0] // 2)])
    drains.append((WUP, peer_up.at[pl.ds(0, up.shape[0] // 2)]))
    send(peer_up.at[half_up], peer_up.at[half_up], FUP, sibling)
    wait_on(recv_sem.at[WDN], peer_down.at[pl.ds(0, hidden // 2)])
    drains.append((WDN, peer_down.at[pl.ds(0, hidden // 2)]))
    send(peer_down.at[half_dn], peer_down.at[half_dn], FDN, sibling)

    arrived(HW, hw_recv.at[pl.ds(0, groups - 1)])
    whole_head = hw_recv[...].reshape(total_channels, C)
    head_sums = column_sums(whole_head)
    own_head = dot(down[...], whole_head).astype(BF16)
    arrived(FUP, peer_up.at[pl.ds(0, up.shape[0] // 2)])
    peer_sums = column_sums(peer_up[...])
    arrived(FDN, peer_down.at[pl.ds(0, hidden // 2)])
    peer_head = dot(peer_down[...], whole_head).astype(BF16)
    arrived(ST2, st2_recv.at[pl.ds(0, groups - 1)])
    sent = [[whole_row(st2_recv[g], i) for i in range(3)] for g in range(groups)]
    mean = jnp.zeros((1, width), F32)
    for row_mean, row_sum, _ in sent:
        mean = mean + (row_mean + row_sum * (1.0 / C))
    mean = mean * (1.0 / groups)
    offsets = [row_mean - mean for row_mean, _, _ in sent]
    square = jnp.zeros((1, width), F32)
    for offset, (_, row_sum, row_square) in zip(offsets, sent):
        square = square + (row_square + 2.0 * offset * row_sum + float(C) * offset * offset)
    scale = lax.rsqrt(square / total_channels + epsilon)
    local_means = in_parts([row_mean for row_mean, _, _ in sent], width)
    offsets = in_parts(offsets, width)
    scale = columns_of([scale], width)[:, 0:1]

    other = weight_peer[1]
    pairs = groups // 2
    for t in parts:
        rows_at = slice(cuts[t] * tile, cuts[t + 1] * tile)
        part = pl.ds(rows_at.start, rows_at.stop - rows_at.start)
        arrived(Y[t], y_recv.at[pl.ds(0, groups - 1), part])
        flat = jnp.concatenate([y_recv[g, rows_at] for g in range(groups)], axis=1)

        def hidden_of(weights, sums):
            shift = dot(offsets[rows_at], sums)
            return gelu((dot(flat, weights) + shift) * scale[rows_at]).astype(BF16)

        hid_own = hidden_of(up[...], own_sums)
        hid_peer = hidden_of(peer_up[...], peer_sums)

        velocity = dot(hid_own, own_head) + dot(hid_peer, peer_head)
        tiles = range(cuts[t], cuts[t + 1])
        vf_send[tiles.start : tiles.stop] = velocity.astype(BF16).reshape(len(tiles), tile, C)
        for g in tiles:

            @pl.when(grp != g)
            def _():
                send(vf_send.at[g], vf_recv.at[grp], VF, (row, g))

        for i in range(pairs):
            pair = lax.rem(grp // 2 + 1 + i, pairs)
            columns = pl.ds(pl.multiple_of(pair * 2 * C, 2 * C), 2 * C)
            partial = dot(hid_own, down[:, columns]) + dot(hid_peer, peer_down[:, columns])
            partial = partial.astype(BF16)
            rs_send[2 * pair, rows_at] = partial[:, :C]
            rs_send[2 * pair + 1, rows_at] = partial[:, C:]
            if i < pairs - 1:
                for g in (2 * pair, 2 * pair + 1):
                    send(rs_send.at[g, part], rs_recv.at[grp, part], RS, (row, g))
        send(rs_send.at[other, part], rs_recv.at[grp, part], RS, (row, other))
    vf_recv[grp] = vf_send[grp]

    mine_at = pl.ds(pl.multiple_of((grp // 2) * 2 * tile, 2 * tile), 2 * tile)
    flat = jnp.concatenate([y_recv[g, mine_at] for g in range(groups)], axis=1)
    means[...] = local_means
    velocity = dot(flat, whole_head) + dot(means[mine_at], head_sums)
    vm_send[...] = velocity.astype(BF16).reshape(2, tile, C)
    send(vm_send.at[1 - side], vm_recv.at[side], VM, (row, other))
    vm_recv[side] = vm_send[side]
    rs_recv[grp] = rs_send[grp]

    for at, halo in ((HUP, halo_up), (HDN, halo_down), (HLF, halo_left), (HRT, halo_right)):
        arrived(at, halo)
    tile_rows = now.shape[1]
    row_at = lax.broadcasted_iota(jnp.int32, (tile_rows, lanes), 0)
    lane_at = lax.broadcasted_iota(jnp.int32, (tile_rows, lanes), 1)
    own = [now[0], now[1]]
    base = []
    for comp in range(2):
        above = jnp.where(row == 0, 0.0, halo_up[comp, 7:8, :])
        below = jnp.where(row == rows - 1, 0.0, halo_down[comp, 0:1, :])
        left = jnp.where(grp == 0, 0.0, halo_left[comp, :, C - 1 : C])
        right = jnp.where(grp == groups - 1, 0.0, halo_right[comp, :, 0:1])
        center = own[comp]
        up_shift = jnp.where(row_at == tile_rows - 1, below, jnp.roll(center, -1, axis=0))
        down_shift = jnp.where(row_at == 0, above, jnp.roll(center, 1, axis=0))
        from_right = jnp.where(lane_at == lanes - 1, right, jnp.roll(center, -1, axis=1))
        from_left = jnp.where(lane_at == 0, left, jnp.roll(center, 1, axis=1))
        laplace = up_shift + down_shift + from_right + from_left - 4.0 * center
        rotated = own[1] if comp == 0 else -own[0]
        base.append(center + time_step * (coriolis * rotated + viscosity * laplace))

    arrived(VF, vf_recv.at[pl.ds(0, groups - 1)])
    arrived(VM, vm_recv.at[0])
    velocity = []
    for r in range(2):
        values = vm_recv[r].astype(F32)
        for g in range(r, groups, 2):
            values = values + vf_recv[g].astype(F32)
        velocity.append(values)
    velocity.append(jnp.zeros((C - 2 * tile, C), F32))
    velocity = jnp.concatenate(velocity, axis=0).T

    wide = 2 * lanes
    source = lax.broadcasted_iota(jnp.int32, (C, wide), 0)
    target = lax.broadcasted_iota(jnp.int32, (C, wide), 1) // PATCH
    spread = jnp.where(source == target, 1.0, 0.0).astype(BF16)
    vel_hi, vel_lo = split_hi_lo(velocity)
    spread_out = dot(vel_hi, spread) + dot(vel_lo, spread)
    x_row = lax.broadcasted_iota(jnp.int32, (C, wide), 0) % PATCH
    x_lane = lax.broadcasted_iota(jnp.int32, (C, wide), 1) % PATCH
    kept = jnp.where(x_row == x_lane, spread_out, 0.0).reshape(C // PATCH, PATCH, wide)
    cells = jnp.sum(kept, axis=1)
    relative = []
    for comp in range(2):
        part = cells[comp * PATCH : (comp + 1) * PATCH]
        ice_vel = jnp.concatenate([part[:, :lanes], part[:, lanes:]], axis=0)
        relative.append(ice_vel - own[comp])
    speed = jnp.sqrt(relative[0] * relative[0] + relative[1] * relative[1] + speed_floor)
    drag = (time_step * drag_coef) * ice[...].astype(F32) * speed
    open_water = land[...].astype(F32)
    for comp in range(2):
        ocean[comp] = open_water * (base[comp] + drag * relative[comp])
    ocean_copy = pltpu.make_async_copy(ocean, oc_hbm, out_sem.at[1])
    ocean_copy.start()

    arrived(RS, rs_recv.at[pl.ds(0, groups - 1)])
    for r in range(2):
        values = rs_recv[r].astype(F32)
        for g in range(r + 2, groups, 2):
            values = values + rs_recv[g].astype(F32)
        bo[r] = (mixed[r] + values).astype(BF16)
    out_copy = pltpu.make_async_copy(bo, bo_hbm, out_sem.at[0])
    out_copy.start()

    for at, like in drains:
        wait_on(send_sem.at[at], like)
    out_copy.wait()
    ocean_copy.wait()


def in_parts(rows, width):
    top = stack_rows(rows, 8, width)
    values = jnp.concatenate([top, top, top, jnp.zeros((C - 24, width), F32)], axis=0).T
    hi, lo = split_hi_lo(values)
    lane = lax.broadcasted_iota(jnp.int32, values.shape, 1)
    return jnp.where((lane >= 8) & (lane < 16), lo.astype(F32), hi.astype(F32)).astype(BF16)


def copy_kernel(bo_in, oc_in, bo_out, oc_out, bo, oc, sem):
    loads = [pltpu.make_async_copy(bo_in, bo, sem.at[0]), pltpu.make_async_copy(oc_in, oc, sem.at[1])]
    stores = [pltpu.make_async_copy(bo, bo_out, sem.at[2]), pltpu.make_async_copy(oc, oc_out, sem.at[3])]
    for load in loads:
        load.start()
    for load, store in zip(loads, stores):
        load.wait()
        store.start()
    for store in stores:
        store.wait()


def body(tokens, spec_first, spec_second, up_weight, down_weight, head_weight, ocean_vel, land_mask, ice_mask):
    rows = lax.axis_size("row")
    groups = lax.axis_size("grp")
    _, width, _ = tokens.shape
    embed, hidden = up_weight.shape
    _, tile_rows, lanes = ocean_vel.shape
    tile = width // groups
    tables = jnp.asarray(dft_tables(rows))
    args = (
        tokens, spec_first, spec_second, up_weight, down_weight, head_weight, ocean_vel, land_mask, ice_mask, tables,
    )
    copies = [pltpu.VMEM(a.shape, a.dtype) for a in args]
    scratch = copies + [
        pltpu.VMEM((8, width // 2), F32),
        pltpu.VMEM((groups, 8, width // 2), F32),
        pltpu.VMEM((rows, 8, C), BF16),
        pltpu.VMEM((rows, 8, C), BF16),
        pltpu.VMEM((rows, 8, C), BF16),
        pltpu.VMEM((rows, 8, C), BF16),
        pltpu.VMEM((2, width, C), F32),
        pltpu.VMEM((2, width, C), BF16),
        pltpu.VMEM((groups, width, C), BF16),
        pltpu.VMEM((2, 8, width // 2), F32),
        pltpu.VMEM((groups, 8, width // 2), F32),
        pltpu.VMEM((embed, hidden), BF16),
        pltpu.VMEM((hidden, embed), BF16),
        pltpu.VMEM((groups, width, C), BF16),
        pltpu.VMEM((groups, width, C), BF16),
        pltpu.VMEM((2, width, C), BF16),
        pltpu.VMEM((width, C), BF16),
        pltpu.VMEM((2, tile, C), BF16),
        pltpu.VMEM((2, tile, C), BF16),
        pltpu.VMEM((groups, tile, C), BF16),
        pltpu.VMEM((groups, tile, C), BF16),
        pltpu.VMEM((groups, C, C), BF16),
        pltpu.VMEM((2, tile_rows, lanes), F32),
        pltpu.VMEM((2, 8, lanes), F32),
        pltpu.VMEM((2, 8, lanes), F32),
        pltpu.VMEM((2, tile_rows, C), F32),
        pltpu.VMEM((2, tile_rows, C), F32),
        pltpu.VMEM((2, tile_rows, lanes), F32),
        pltpu.SemaphoreType.DMA((len(args) + 3,)),
        pltpu.SemaphoreType.DMA((19,)),
        pltpu.SemaphoreType.DMA((19,)),
        pltpu.SemaphoreType.DMA((2,)),
    ]
    outs = (
        jax.ShapeDtypeStruct(tokens.shape, BF16),
        jax.ShapeDtypeStruct(ocean_vel.shape, F32),
    )
    results = pl.pallas_call(
        functools.partial(kernel, rows, groups),
        out_shape=outs,
        in_specs=[pl.BlockSpec(memory_space=pl.ANY)] * len(args),
        out_specs=[pl.BlockSpec(memory_space=pl.ANY)] * 2,
        scratch_shapes=scratch,
        compiler_params=pltpu.CompilerParams(
            collective_id=0, has_side_effects=True, vmem_limit_bytes=60 * 1024 * 1024
        ),
    )(*args)
    return pl.pallas_call(
        copy_kernel,
        out_shape=outs,
        in_specs=[pl.BlockSpec(memory_space=pl.ANY)] * 2,
        out_specs=[pl.BlockSpec(memory_space=pl.ANY)] * 2,
        scratch_shapes=[pltpu.VMEM(out.shape, out.dtype) for out in outs] + [pltpu.SemaphoreType.DMA((4,))],
    )(*results)


def solution(mesh):
    placed = (
        P("row", None, "grp"),
        P(None, "grp", None),
        P(None, "grp", None),
        P(None, "grp"),
        P("grp", None),
        P("grp", None),
        P(None, "row", "grp"),
        P("row", "grp"),
        P("row", "grp"),
    )
    return jax.shard_map(
        body,
        mesh=mesh,
        in_specs=placed,
        out_specs=(P("row", None, "grp"), P(None, "row", "grp")),
        check_vma=False,
    )
```

```python
import functools
import math

import jax
import jax.numpy as jnp
import ml_dtypes
import numpy as np
from jax import lax
from jax.experimental import pallas as pl
from jax.experimental.pallas import tpu as pltpu
from jax.sharding import PartitionSpec as P

PATCH = 8
C = 128

epsilon = 1e-05
shrink_level = 0.01
drag_coef = 0.25
time_step = 0.5
coriolis = 0.3
viscosity = 1.0
speed_floor = 0.01

F32 = jnp.float32
BF16 = jnp.bfloat16
MESH = pl.DeviceIdType.MESH


def dft_tables(rows):
    height, width = 2 * rows, 4 * rows
    d, r, kk, part = (v.reshape(-1, 1) for v in np.meshgrid(range(rows), range(2), range(2), range(2), indexing="ij"))
    k = 2 * d + kk
    r_col, w = (v.reshape(1, -1) for v in np.meshgrid(range(2), range(width), indexing="ij"))
    angle = 2.0 * np.pi * ((k * w) % width) / width
    row_fwd = np.where(r == r_col, np.where(part == 0, np.cos(angle), -np.sin(angle)), 0.0)
    row_bwd = (np.where(k == 0, 1.0, 2.0) * row_fwd).T
    kk_row, part_row, a = (
        v.reshape(-1, 1) for v in np.meshgrid(range(2), range(2), range(height), indexing="ij")
    )
    h, kk, part = (2 * d + r).T, kk.T, part.T
    angle = 2.0 * np.pi * ((a * h) % height) / height
    cos, sin = np.cos(angle), np.sin(angle)
    real = np.where(part == 0, cos, sin)
    imag = np.where(part == 0, -sin, cos)
    col_fwd = np.where(kk_row == kk, np.where(part_row == 0, real, imag), 0.0)
    return np.stack([row_fwd, col_fwd, col_fwd.T, row_bwd]).astype(ml_dtypes.bfloat16)


def dot(a, b):
    return jnp.dot(a, b, preferred_element_type=F32)


def dot_nt(a, b):
    return lax.dot_general(a, b, (((1,), (1,)), ((), ())), preferred_element_type=F32)


def split_hi_lo(values):
    hi = values.astype(BF16)
    return hi, (values - hi.astype(F32)).astype(BF16)


def soft_shrink(values):
    return values - jnp.clip(values, -shrink_level, shrink_level)


def gelu(values):
    return 0.5 * values * (1.0 + lax.erf(values * (1.0 / math.sqrt(2.0))))


def far_first(count):
    return sorted(range(1, count), key=lambda i: -min(i, count - i))


def complex_matrix(ref):
    real, imag = ref[0], ref[1]
    top = jnp.concatenate([real, imag], axis=1)
    low = jnp.concatenate([-imag, real], axis=1)
    return jnp.concatenate([top, low], axis=0)


def stack_rows(rows, count, width):
    at = lax.broadcasted_iota(jnp.int32, (count, width), 0)
    out = jnp.zeros((count, width), F32)
    for i, values in enumerate(rows):
        out = jnp.where(at == i, values, out)
    return out


def stack_halves(rows, width):
    half = width // 2
    return stack_rows([part for values in rows for part in (values[:, :half], values[:, half:])], 8, half)


def whole_row(values, i):
    return jnp.concatenate([values[2 * i : 2 * i + 1], values[2 * i + 1 : 2 * i + 2]], axis=1)


def columns_of(rows, width):
    top = stack_rows(rows, 8, width)
    return jnp.concatenate([top, jnp.zeros((C - 8, width), F32)], axis=0).T


def kernel(
    rows,
    groups,
    tok_hbm, first_hbm, second_hbm, up_hbm, down_hbm, head_hbm, vel_hbm, land_hbm, ice_hbm, tab_hbm,
    bo_hbm, oc_hbm,
    tok, first, second, up, down, head, vel, land, ice, tab,
    st1_send, st1_recv, z1_send, z1_recv, z2_send, z2_recv,
    mixed, y_send, y_recv, st2_send, st2_recv, peer_up, peer_down, rs_send, rs_recv,
    bo, means, vm_send, vm_recv, vf_send, vf_recv, hw_recv, now, halo_up, halo_down, halo_left, halo_right, ocean,
    local_sem, send_sem, recv_sem, out_sem,
):
    width = tok.shape[1]
    total_channels = C * groups
    row, grp = lax.axis_index("row"), lax.axis_index("grp")
    core, side = row % 2, grp % 2
    hidden = up.shape[1]

    tok_load = pltpu.make_async_copy(tok_hbm, tok, local_sem.at[0])
    tok_load.start()
    weight_peer = (row, grp + 1 - 2 * side)
    sibling = (row + 1 - 2 * core, grp)
    r_peers = [lax.rem(row + i, rows) for i in far_first(rows)]
    planes = rows // 4
    z, y_lo = row // 4, (row // 2) % 2
    far_planes = [lax.rem(z + i, planes) * 4 for i in far_first(planes)]
    staged_peers = []
    for to_core in range(2):
        staged_peers += [z_at + 2 * y_at + to_core for z_at in far_planes for y_at in range(2)]
        staged_peers.append(z * 4 + 2 * (1 - y_lo) + to_core)
    staged_peers.append(sibling[0])
    g_peers = [lax.rem(grp + i, groups) for i in far_first(groups)]
    row_above, row_below = lax.rem(row + rows - 1, rows), lax.rem(row + 1, rows)
    greeted = [(r, grp) for r in r_peers] + [(row, g) for g in g_peers]
    barrier = pltpu.get_barrier_semaphore()
    for peer in greeted:
        pl.semaphore_signal(barrier, inc=1, device_id=peer, device_id_type=MESH)

    loads = {"tok": tok_load}
    for i, (name, src, dst) in enumerate(
        [
            ("vel", vel_hbm, vel),
            ("land", land_hbm, land),
            ("head", head_hbm, head),
            ("tab0", tab_hbm.at[0], tab.at[0]),
            ("first", first_hbm, first),
            ("second", second_hbm, second),
            ("tab1", tab_hbm.at[1], tab.at[1]),
            ("tab2", tab_hbm.at[2], tab.at[2]),
            ("tab3", tab_hbm.at[3], tab.at[3]),
            ("up", up_hbm, up),
            ("down", down_hbm, down),
            ("ice", ice_hbm, ice),
        ]
    ):
        loads[name] = pltpu.make_async_copy(src, dst, local_sem.at[i + 1])
        loads[name].start()

    ones = jnp.ones((16, C), BF16)
    loads["tok"].wait()
    sums = []
    squares = []
    for r in range(2):
        values = tok[r]
        wide = values.astype(F32)
        hi, lo = split_hi_lo(wide * wide)
        sums.append(dot_nt(ones, values)[0:1])
        squares.append((dot_nt(ones, hi) + dot_nt(ones, lo))[0:1])
    st1_send[...] = stack_halves(sums + squares, width)
    st1_recv[grp] = st1_send[...]
    loads["head"].wait()
    hw_recv[grp] = head[...]
    loads["vel"].wait()
    loads["land"].wait()
    open_water = land[...].astype(F32)
    now[0] = vel[0] * open_water
    now[1] = vel[1] * open_water

    pl.semaphore_wait(barrier, len(greeted))

    drains = []

    def send(src, dst, at, peer):
        pltpu.make_async_remote_copy(
            src_ref=src,
            dst_ref=dst,
            send_sem=send_sem.at[at],
            recv_sem=recv_sem.at[at],
            device_id=peer,
            device_id_type=MESH,
        ).start()

    def wait_on(sem, like):
        pltpu.make_async_copy(like, like, sem).wait()

    def arrived(at, like):
        wait_on(recv_sem.at[at], like)
        drains.append((at, like))

    ST1, WUP, WDN, HW, HUP, HDN, HLF, HRT, ST2, FUP, FDN, RS, VF, VM = range(14)
    Z1, Z2, Y = 14, 15, (16, 17, 18, 19)

    for g in g_peers:
        send(st1_send, st1_recv.at[grp], ST1, (row, g))
    half_up = pl.ds(pl.multiple_of(core * (up.shape[0] // 2), up.shape[0] // 2), up.shape[0] // 2)
    half_dn = pl.ds(pl.multiple_of(core * (hidden // 2), hidden // 2), hidden // 2)
    send(up_hbm.at[half_up], peer_up.at[half_up], WUP, weight_peer)
    send(down_hbm.at[half_dn], peer_down.at[half_dn], WDN, weight_peer)

    arrived(ST1, st1_recv.at[pl.ds(0, groups - 1)])
    totals = st1_recv[0]
    for g in range(1, groups):
        totals = totals + st1_recv[g]
    totals = totals / total_channels
    mean = [whole_row(totals, r) for r in range(2)]
    scale = [lax.rsqrt(whole_row(totals, 2 + r) - mean[r] * mean[r] + epsilon) for r in range(2)]
    stats = columns_of(mean + scale, width)
    loads["tab0"].wait()
    normed = []
    for r in range(2):
        inputs = tok[r].astype(F32)
        normed.append((inputs - stats[:, r : r + 1]) * stats[:, 2 + r : 3 + r])
        mixed[r] = inputs + normed[r]

    height, size = 2 * rows, 8 * rows
    row_scale, col_scale = 1.0 / math.sqrt(width), 1.0 / math.sqrt(height)
    flat = jnp.concatenate([normed[0].astype(BF16), normed[1].astype(BF16)], axis=0)
    z1_send[...] = (dot(tab[0], flat) * row_scale).reshape(rows, 8, C).astype(BF16)
    for r in staged_peers:
        send(z1_send.at[r], z1_recv.at[row], Z1, (r, grp))
    z1_recv[row] = z1_send[row]

    for g in g_peers:
        send(head, hw_recv.at[grp], HW, (row, g))
    send(now.at[:, pl.ds(8, 8)], halo_up, HUP, (row_below, grp))
    send(now.at[:, pl.ds(0, 8)], halo_down, HDN, (row_above, grp))
    lanes = now.shape[2]
    send(now.at[:, :, pl.ds(lanes - C, C)], halo_left, HLF, (row, lax.rem(grp + 1, groups)))
    send(now.at[:, :, pl.ds(0, C)], halo_right, HRT, (row, lax.rem(grp + groups - 1, groups)))
    loads["first"].wait()
    loads["second"].wait()
    weight_one = complex_matrix(first).astype(BF16)
    weight_two, weight_two_lo = split_hi_lo(complex_matrix(second))
    loads["up"].wait()
    loads["down"].wait()
    loads["ice"].wait()
    for i in range(1, 4):
        loads["tab" + str(i)].wait()
    block_at = lax.broadcasted_iota(jnp.int32, (16, total_channels), 0) % 8
    block_of = lax.broadcasted_iota(jnp.int32, (16, total_channels), 1) // C
    pick = jnp.where(block_at == block_of, 1.0, 0.0).astype(BF16)

    def column_sums(weights):
        hi, lo = split_hi_lo(dot(pick, weights))
        return jnp.concatenate([hi[:16], lo, jnp.zeros((C - 32, weights.shape[1]), BF16)], axis=0)

    own_sums = column_sums(up[...])

    def blocks(values):
        return [values[i * height : (i + 1) * height] for i in range(4)]

    arrived(Z1, z1_recv.at[pl.ds(0, rows - 1)])
    columns = z1_recv[...].astype(F32).reshape(size, C).astype(BF16)
    freq = blocks((dot(tab[1], columns) * col_scale).astype(BF16))
    freq = jnp.concatenate(
        [jnp.concatenate(freq[:2], axis=1), jnp.concatenate(freq[2:], axis=1)], axis=0
    )
    hid = jax.nn.relu(dot(freq, weight_one)).astype(BF16)
    mix = soft_shrink(dot(hid, weight_two) + dot(hid, weight_two_lo)).astype(BF16)
    mix = jnp.concatenate(
        [mix[kk * height : (kk + 1) * height, p * C : (p + 1) * C] for kk in range(2) for p in range(2)], axis=0
    )
    z2_send[...] = (dot(tab[2], mix) * col_scale).reshape(rows, 8, C).astype(BF16)
    for r in r_peers:
        send(z2_send.at[r], z2_recv.at[row], Z2, (r, grp))
    z2_recv[row] = z2_send[row]

    arrived(Z2, z2_recv.at[pl.ds(0, rows - 1)])
    columns = z2_recv[...].astype(F32).reshape(size, C).astype(BF16)
    square_ones = jnp.ones((C, C), BF16)
    for r in range(2):
        values = mixed[r] + dot(tab[3, r * width : (r + 1) * width], columns) * row_scale
        mixed[r] = values
        hi = values.astype(BF16)
        local_mean = dot(hi, square_ones) * (1.0 / C)
        centered = (values - local_mean).astype(BF16)
        y_send[r] = centered
        wide = centered.astype(F32)
        row_mean = dot_nt(ones, hi)[0:1] * (1.0 / C)
        row_sum = dot_nt(ones, centered)[0:1]
        sq_hi, sq_lo = split_hi_lo(wide * wide)
        row_square = (dot_nt(ones, sq_hi) + dot_nt(ones, sq_lo))[0:1]
        st2_send[r] = stack_halves([row_mean, row_sum, row_square], width)
    for g in g_peers:
        send(st2_send.at[g % 2], st2_recv.at[grp], ST2, (row, g))
    tile = width // groups
    cuts = (0, 1, 3, 5, 8) if groups == 8 else (0, groups // 2, groups)
    parts = range(len(cuts) - 1)
    for t in parts:
        tokens_at = pl.ds(cuts[t] * tile, (cuts[t + 1] - cuts[t]) * tile)
        for g in g_peers:
            send(y_send.at[g % 2, tokens_at], y_recv.at[grp, tokens_at], Y[t], (row, g))
    y_recv[grp] = y_send[side]
    st2_recv[grp] = st2_send[side]

    wait_on(recv_sem.at[WUP], peer_up.at[pl.ds(0, up.shape[0] // 2)])
    drains.append((WUP, peer_up.at[pl.ds(0, up.shape[0] // 2)]))
    send(peer_up.at[half_up], peer_up.at[half_up], FUP, sibling)
    wait_on(recv_sem.at[WDN], peer_down.at[pl.ds(0, hidden // 2)])
    drains.append((WDN, peer_down.at[pl.ds(0, hidden // 2)]))
    send(peer_down.at[half_dn], peer_down.at[half_dn], FDN, sibling)

    arrived(HW, hw_recv.at[pl.ds(0, groups - 1)])
    whole_head = hw_recv[...].reshape(total_channels, C)
    head_sums = column_sums(whole_head)
    own_head = dot(down[...], whole_head).astype(BF16)
    arrived(FUP, peer_up.at[pl.ds(0, up.shape[0] // 2)])
    peer_sums = column_sums(peer_up[...])
    arrived(FDN, peer_down.at[pl.ds(0, hidden // 2)])
    peer_head = dot(peer_down[...], whole_head).astype(BF16)
    arrived(ST2, st2_recv.at[pl.ds(0, groups - 1)])
    sent = [[whole_row(st2_recv[g], i) for i in range(3)] for g in range(groups)]
    mean = jnp.zeros((1, width), F32)
    for row_mean, row_sum, _ in sent:
        mean = mean + (row_mean + row_sum * (1.0 / C))
    mean = mean * (1.0 / groups)
    offsets = [row_mean - mean for row_mean, _, _ in sent]
    square = jnp.zeros((1, width), F32)
    for offset, (_, row_sum, row_square) in zip(offsets, sent):
        square = square + (row_square + 2.0 * offset * row_sum + float(C) * offset * offset)
    scale = lax.rsqrt(square / total_channels + epsilon)
    local_means = in_parts([row_mean for row_mean, _, _ in sent], width)
    offsets = in_parts(offsets, width)
    scale = columns_of([scale], width)[:, 0:1]

    other = weight_peer[1]
    for t in parts:
        rows_at = slice(cuts[t] * tile, cuts[t + 1] * tile)
        part = pl.ds(rows_at.start, rows_at.stop - rows_at.start)
        arrived(Y[t], y_recv.at[pl.ds(0, groups - 1), part])
        flat = jnp.concatenate([y_recv[g, rows_at] for g in range(groups)], axis=1)

        def hidden_of(weights, sums):
            shift = dot(offsets[rows_at], sums)
            return gelu((dot(flat, weights) + shift) * scale[rows_at]).astype(BF16)

        hid_own = hidden_of(up[...], own_sums)
        hid_peer = hidden_of(peer_up[...], peer_sums)

        partial = (dot(hid_own, down[...]) + dot(hid_peer, peer_down[...])).astype(BF16)
        velocity = dot(hid_own, own_head) + dot(hid_peer, peer_head)
        for g in range(groups):
            rs_send[g, rows_at] = partial[:, g * C : (g + 1) * C]
        tiles = range(cuts[t], cuts[t + 1])
        vf_send[tiles.start : tiles.stop] = velocity.astype(BF16).reshape(len(tiles), tile, C)
        for g in tiles:

            @pl.when(grp != g)
            def _():
                send(vf_send.at[g], vf_recv.at[grp], VF, (row, g))

        for i in range(1, groups // 2):
            pair = lax.rem(grp // 2 + i, groups // 2)
            for g in (2 * pair, 2 * pair + 1):
                send(rs_send.at[g, part], rs_recv.at[grp, part], RS, (row, g))
        send(rs_send.at[other, part], rs_recv.at[grp, part], RS, (row, other))
    vf_recv[grp] = vf_send[grp]

    mine_at = pl.ds(pl.multiple_of((grp // 2) * 2 * tile, 2 * tile), 2 * tile)
    flat = jnp.concatenate([y_recv[g, mine_at] for g in range(groups)], axis=1)
    means[...] = local_means
    velocity = dot(flat, whole_head) + dot(means[mine_at], head_sums)
    vm_send[...] = velocity.astype(BF16).reshape(2, tile, C)
    send(vm_send.at[1 - side], vm_recv.at[side], VM, (row, other))
    vm_recv[side] = vm_send[side]
    rs_recv[grp] = rs_send[grp]

    for at, halo in ((HUP, halo_up), (HDN, halo_down), (HLF, halo_left), (HRT, halo_right)):
        arrived(at, halo)
    tile_rows = now.shape[1]
    row_at = lax.broadcasted_iota(jnp.int32, (tile_rows, lanes), 0)
    lane_at = lax.broadcasted_iota(jnp.int32, (tile_rows, lanes), 1)
    own = [now[0], now[1]]
    base = []
    for comp in range(2):
        above = jnp.where(row == 0, 0.0, halo_up[comp, 7:8, :])
        below = jnp.where(row == rows - 1, 0.0, halo_down[comp, 0:1, :])
        left = jnp.where(grp == 0, 0.0, halo_left[comp, :, C - 1 : C])
        right = jnp.where(grp == groups - 1, 0.0, halo_right[comp, :, 0:1])
        center = own[comp]
        up_shift = jnp.where(row_at == tile_rows - 1, below, jnp.roll(center, -1, axis=0))
        down_shift = jnp.where(row_at == 0, above, jnp.roll(center, 1, axis=0))
        from_right = jnp.where(lane_at == lanes - 1, right, jnp.roll(center, -1, axis=1))
        from_left = jnp.where(lane_at == 0, left, jnp.roll(center, 1, axis=1))
        laplace = up_shift + down_shift + from_right + from_left - 4.0 * center
        rotated = own[1] if comp == 0 else -own[0]
        base.append(center + time_step * (coriolis * rotated + viscosity * laplace))

    arrived(VF, vf_recv.at[pl.ds(0, groups - 1)])
    arrived(VM, vm_recv.at[0])
    velocity = []
    for r in range(2):
        values = vm_recv[r].astype(F32)
        for g in range(r, groups, 2):
            values = values + vf_recv[g].astype(F32)
        velocity.append(values)
    velocity.append(jnp.zeros((C - 2 * tile, C), F32))
    velocity = jnp.concatenate(velocity, axis=0).T

    wide = 2 * lanes
    source = lax.broadcasted_iota(jnp.int32, (C, wide), 0)
    target = lax.broadcasted_iota(jnp.int32, (C, wide), 1) // PATCH
    spread = jnp.where(source == target, 1.0, 0.0).astype(BF16)
    vel_hi, vel_lo = split_hi_lo(velocity)
    spread_out = dot(vel_hi, spread) + dot(vel_lo, spread)
    x_row = lax.broadcasted_iota(jnp.int32, (C, wide), 0) % PATCH
    x_lane = lax.broadcasted_iota(jnp.int32, (C, wide), 1) % PATCH
    kept = jnp.where(x_row == x_lane, spread_out, 0.0).reshape(C // PATCH, PATCH, wide)
    cells = jnp.sum(kept, axis=1)
    relative = []
    for comp in range(2):
        part = cells[comp * PATCH : (comp + 1) * PATCH]
        ice_vel = jnp.concatenate([part[:, :lanes], part[:, lanes:]], axis=0)
        relative.append(ice_vel - own[comp])
    speed = jnp.sqrt(relative[0] * relative[0] + relative[1] * relative[1] + speed_floor)
    drag = (time_step * drag_coef) * ice[...].astype(F32) * speed
    open_water = land[...].astype(F32)
    for comp in range(2):
        ocean[comp] = open_water * (base[comp] + drag * relative[comp])
    out_copies = []
    ocean_copy = pltpu.make_async_copy(ocean, oc_hbm, out_sem.at[2])
    ocean_copy.start()

    arrived(RS, rs_recv.at[pl.ds(0, groups - 1)])
    for r in range(2):
        values = rs_recv[r].astype(F32)
        for g in range(r + 2, groups, 2):
            values = values + rs_recv[g].astype(F32)
        bo[r] = (mixed[r] + values).astype(BF16)
        out_copies.append(pltpu.make_async_copy(bo.at[r], bo_hbm.at[r], out_sem.at[r]))
        out_copies[r].start()

    for at, like in drains:
        wait_on(send_sem.at[at], like)
    for copy in out_copies + [ocean_copy]:
        copy.wait()


def in_parts(rows, width):
    top = stack_rows(rows, 8, width)
    values = jnp.concatenate([top, top, top, jnp.zeros((C - 24, width), F32)], axis=0).T
    hi, lo = split_hi_lo(values)
    lane = lax.broadcasted_iota(jnp.int32, values.shape, 1)
    return jnp.where((lane >= 8) & (lane < 16), lo.astype(F32), hi.astype(F32)).astype(BF16)


def quarters(ref):
    half = ref.shape[1] // 2
    return [ref.at[i, pl.ds(j * half, half)] for i in range(2) for j in range(2)]


def copy_kernel(bo_in, oc_in, bo_out, oc_out, bo, oc, sem):
    steps = list(zip(quarters(bo_in), quarters(bo), quarters(bo_out))) + [(oc_in, oc, oc_out)]
    loads = [pltpu.make_async_copy(src, mid, sem.at[0, i]) for i, (src, mid, _) in enumerate(steps)]
    stores = [pltpu.make_async_copy(mid, dst, sem.at[1, i]) for i, (_, mid, dst) in enumerate(steps)]
    for load in loads:
        load.start()
    for load, store in zip(loads, stores):
        load.wait()
        store.start()
    for store in stores:
        store.wait()


def body(tokens, spec_first, spec_second, up_weight, down_weight, head_weight, ocean_vel, land_mask, ice_mask):
    rows = lax.axis_size("row")
    groups = lax.axis_size("grp")
    _, width, _ = tokens.shape
    embed, hidden = up_weight.shape
    _, tile_rows, lanes = ocean_vel.shape
    tile = width // groups
    tables = jnp.asarray(dft_tables(rows))
    args = (
        tokens, spec_first, spec_second, up_weight, down_weight, head_weight, ocean_vel, land_mask, ice_mask, tables,
    )
    copies = [pltpu.VMEM(a.shape, a.dtype) for a in args]
    scratch = copies + [
        pltpu.VMEM((8, width // 2), F32),
        pltpu.VMEM((groups, 8, width // 2), F32),
        pltpu.VMEM((rows, 8, C), BF16),
        pltpu.VMEM((rows, 8, C), BF16),
        pltpu.VMEM((rows, 8, C), BF16),
        pltpu.VMEM((rows, 8, C), BF16),
        pltpu.VMEM((2, width, C), F32),
        pltpu.VMEM((2, width, C), BF16),
        pltpu.VMEM((groups, width, C), BF16),
        pltpu.VMEM((2, 8, width // 2), F32),
        pltpu.VMEM((groups, 8, width // 2), F32),
        pltpu.VMEM((embed, hidden), BF16),
        pltpu.VMEM((hidden, embed), BF16),
        pltpu.VMEM((groups, width, C), BF16),
        pltpu.VMEM((groups, width, C), BF16),
        pltpu.VMEM((2, width, C), BF16),
        pltpu.VMEM((width, C), BF16),
        pltpu.VMEM((2, tile, C), BF16),
        pltpu.VMEM((2, tile, C), BF16),
        pltpu.VMEM((groups, tile, C), BF16),
        pltpu.VMEM((groups, tile, C), BF16),
        pltpu.VMEM((groups, C, C), BF16),
        pltpu.VMEM((2, tile_rows, lanes), F32),
        pltpu.VMEM((2, 8, lanes), F32),
        pltpu.VMEM((2, 8, lanes), F32),
        pltpu.VMEM((2, tile_rows, C), F32),
        pltpu.VMEM((2, tile_rows, C), F32),
        pltpu.VMEM((2, tile_rows, lanes), F32),
        pltpu.SemaphoreType.DMA((len(args) + 3,)),
        pltpu.SemaphoreType.DMA((20,)),
        pltpu.SemaphoreType.DMA((20,)),
        pltpu.SemaphoreType.DMA((3,)),
    ]
    outs = (
        jax.ShapeDtypeStruct(tokens.shape, BF16),
        jax.ShapeDtypeStruct(ocean_vel.shape, F32),
    )
    results = pl.pallas_call(
        functools.partial(kernel, rows, groups),
        out_shape=outs,
        in_specs=[pl.BlockSpec(memory_space=pl.ANY)] * len(args),
        out_specs=[pl.BlockSpec(memory_space=pl.ANY)] * 2,
        scratch_shapes=scratch,
        compiler_params=pltpu.CompilerParams(
            collective_id=0, has_side_effects=True, vmem_limit_bytes=60 * 1024 * 1024
        ),
    )(*args)
    return pl.pallas_call(
        copy_kernel,
        out_shape=outs,
        in_specs=[pl.BlockSpec(memory_space=pl.ANY)] * 2,
        out_specs=[pl.BlockSpec(memory_space=pl.ANY)] * 2,
        scratch_shapes=[pltpu.VMEM(out.shape, out.dtype) for out in outs] + [pltpu.SemaphoreType.DMA((2, 5))],
    )(*results)


def solution(mesh):
    placed = (
        P("row", None, "grp"),
        P(None, "grp", None),
        P(None, "grp", None),
        P(None, "grp"),
        P("grp", None),
        P("grp", None),
        P(None, "row", "grp"),
        P("row", "grp"),
        P("row", "grp"),
    )
    return jax.shard_map(
        body,
        mesh=mesh,
        in_specs=placed,
        out_specs=(P("row", None, "grp"), P(None, "row", "grp")),
        check_vma=False,
    )
```

```python
import functools
import math

import jax
import jax.numpy as jnp
import ml_dtypes
import numpy as np
from jax import lax
from jax.experimental import pallas as pl
from jax.experimental.pallas import tpu as pltpu
from jax.sharding import PartitionSpec as P

PATCH = 8
C = 128

epsilon = 1e-05
shrink_level = 0.01
drag_coef = 0.25
time_step = 0.5
coriolis = 0.3
viscosity = 1.0
speed_floor = 0.01

F32 = jnp.float32
BF16 = jnp.bfloat16
MESH = pl.DeviceIdType.MESH


def dft_tables(rows):
    height, width = 2 * rows, 4 * rows
    d, r, kk, part = (v.reshape(-1, 1) for v in np.meshgrid(range(rows), range(2), range(2), range(2), indexing="ij"))
    k = 2 * d + kk
    r_col, w = (v.reshape(1, -1) for v in np.meshgrid(range(2), range(width), indexing="ij"))
    angle = 2.0 * np.pi * ((k * w) % width) / width
    row_fwd = np.where(r == r_col, np.where(part == 0, np.cos(angle), -np.sin(angle)), 0.0)
    row_fwd = row_fwd / math.sqrt(width)
    row_bwd = (np.where(k == 0, 1.0, 2.0) * row_fwd).T
    kk_row, part_row, a = (
        v.reshape(-1, 1) for v in np.meshgrid(range(2), range(2), range(height), indexing="ij")
    )
    h, kk, part = (2 * d + r).T, kk.T, part.T
    angle = 2.0 * np.pi * ((a * h) % height) / height
    cos, sin = np.cos(angle), np.sin(angle)
    real = np.where(part == 0, cos, sin)
    imag = np.where(part == 0, -sin, cos)
    col_fwd = np.where(kk_row == kk, np.where(part_row == 0, real, imag), 0.0)
    return np.stack([row_fwd, col_fwd, col_fwd.T, row_bwd]).astype(ml_dtypes.bfloat16)


def dot(a, b):
    return jnp.dot(a, b, preferred_element_type=F32)


def dot_nt(a, b):
    return lax.dot_general(a, b, (((1,), (1,)), ((), ())), preferred_element_type=F32)


def split_hi_lo(values):
    hi = values.astype(BF16)
    return hi, (values - hi.astype(F32)).astype(BF16)


def soft_shrink(values):
    return values - jnp.clip(values, -shrink_level, shrink_level)


def gelu(values):
    return 0.5 * values * (1.0 + lax.erf(values * (1.0 / math.sqrt(2.0))))


def far_first(count):
    return sorted(range(1, count), key=lambda i: -min(i, count - i))


def complex_matrix(ref):
    real, imag = ref[0], ref[1]
    top = jnp.concatenate([real, imag], axis=1)
    low = jnp.concatenate([-imag, real], axis=1)
    return jnp.concatenate([top, low], axis=0)


def stack_rows(rows, count, width):
    at = lax.broadcasted_iota(jnp.int32, (count, width), 0)
    out = jnp.zeros((count, width), F32)
    for i, values in enumerate(rows):
        out = jnp.where(at == i, values, out)
    return out


def stack_halves(rows, width):
    half = width // 2
    return stack_rows([part for values in rows for part in (values[:, :half], values[:, half:])], 8, half)


def whole_row(values, i):
    return jnp.concatenate([values[2 * i : 2 * i + 1], values[2 * i + 1 : 2 * i + 2]], axis=1)


def columns_of(rows, width):
    top = stack_rows(rows, 8, width)
    return jnp.concatenate([top, jnp.zeros((C - 8, width), F32)], axis=0).T


def kernel(
    rows,
    groups,
    tok_hbm, first_hbm, second_hbm, up_hbm, down_hbm, head_hbm, vel_hbm, land_hbm, ice_hbm, tab_hbm,
    bo_hbm, oc_hbm,
    tok, first, second, up, down, head, vel, land, ice, tab,
    st1_send, st1_recv, z1_send, z1_recv, z2_send, z2_recv,
    mixed, y_send, y_recv, st2_send, st2_recv, peer_up, peer_down, rs_send, rs_recv,
    bo, means, vm_send, vm_recv, vf_send, vf_recv, hw_recv, now, halo_up, halo_down, halo_left, halo_right, ocean,
    local_sem, send_sem, recv_sem, out_sem,
):
    width = tok.shape[1]
    total_channels = C * groups
    row, grp = lax.axis_index("row"), lax.axis_index("grp")
    core, side = row % 2, grp % 2
    hidden = up.shape[1]

    tok_load = pltpu.make_async_copy(tok_hbm, tok, local_sem.at[0])
    tok_load.start()
    weight_peer = (row, grp + 1 - 2 * side)
    sibling = (row + 1 - 2 * core, grp)
    r_peers = [lax.rem(row + i, rows) for i in far_first(rows)]
    planes = rows // 4
    z, y_lo = row // 4, (row // 2) % 2
    far_planes = [lax.rem(z + i, planes) * 4 for i in far_first(planes)]
    staged_peers = []
    for to_core in range(2):
        staged_peers += [z_at + 2 * y_at + to_core for z_at in far_planes for y_at in range(2)]
        staged_peers.append(z * 4 + 2 * (1 - y_lo) + to_core)
    staged_peers.append(sibling[0])
    g_peers = [lax.rem(grp + i, groups) for i in far_first(groups)]
    row_above, row_below = lax.rem(row + rows - 1, rows), lax.rem(row + 1, rows)
    greeted = [(r, grp) for r in r_peers] + [(row, g) for g in g_peers]
    barrier = pltpu.get_barrier_semaphore()
    for peer in greeted:
        pl.semaphore_signal(barrier, inc=1, device_id=peer, device_id_type=MESH)

    loads = {"tok": tok_load}
    for i, (name, src, dst) in enumerate(
        [
            ("vel", vel_hbm, vel),
            ("land", land_hbm, land),
            ("head", head_hbm, head),
            ("tab0", tab_hbm.at[0], tab.at[0]),
            ("first", first_hbm, first),
            ("second", second_hbm, second),
            ("tab1", tab_hbm.at[1], tab.at[1]),
            ("tab2", tab_hbm.at[2], tab.at[2]),
            ("tab3", tab_hbm.at[3], tab.at[3]),
            ("up", up_hbm, up),
            ("down", down_hbm, down),
            ("ice", ice_hbm, ice),
        ]
    ):
        loads[name] = pltpu.make_async_copy(src, dst, local_sem.at[i + 1])
        loads[name].start()

    ones = jnp.ones((16, C), BF16)
    loads["tok"].wait()
    sums = []
    squares = []
    for r in range(2):
        values = tok[r]
        wide = values.astype(F32)
        hi, lo = split_hi_lo(wide * wide)
        sums.append(dot_nt(ones, values)[0:1])
        squares.append((dot_nt(ones, hi) + dot_nt(ones, lo))[0:1])
    st1_send[...] = stack_halves(sums + squares, width)
    st1_recv[grp] = st1_send[...]
    loads["head"].wait()
    hw_recv[grp] = head[...]
    loads["vel"].wait()
    loads["land"].wait()
    open_water = land[...].astype(F32)
    now[0] = vel[0] * open_water
    now[1] = vel[1] * open_water

    pl.semaphore_wait(barrier, len(greeted))

    drains = []

    def send(src, dst, at, peer):
        pltpu.make_async_remote_copy(
            src_ref=src,
            dst_ref=dst,
            send_sem=send_sem.at[at],
            recv_sem=recv_sem.at[at],
            device_id=peer,
            device_id_type=MESH,
        ).start()

    def wait_on(sem, like):
        pltpu.make_async_copy(like, like, sem).wait()

    def arrived(at, like):
        wait_on(recv_sem.at[at], like)
        drains.append((at, like))

    ST1, WUP, WDN, HW, HUP, HDN, HLF, HRT, ST2, FUP, FDN, RS, VF, VM = range(14)
    Z1, Z2, Y = 14, 15, (16, 17, 18, 19)

    for g in g_peers:
        send(st1_send, st1_recv.at[grp], ST1, (row, g))
    half_up = pl.ds(pl.multiple_of(core * (up.shape[0] // 2), up.shape[0] // 2), up.shape[0] // 2)
    half_dn = pl.ds(pl.multiple_of(core * (hidden // 2), hidden // 2), hidden // 2)
    send(up_hbm.at[half_up], peer_up.at[half_up], WUP, weight_peer)
    send(down_hbm.at[half_dn], peer_down.at[half_dn], WDN, weight_peer)

    arrived(ST1, st1_recv.at[pl.ds(0, groups - 1)])
    totals = st1_recv[0]
    for g in range(1, groups):
        totals = totals + st1_recv[g]
    totals = totals / total_channels
    mean = [whole_row(totals, r) for r in range(2)]
    scale = [lax.rsqrt(whole_row(totals, 2 + r) - mean[r] * mean[r] + epsilon) for r in range(2)]
    stats = columns_of(mean + scale, width)
    loads["tab0"].wait()
    normed = []
    for r in range(2):
        inputs = tok[r].astype(F32)
        normed.append((inputs - stats[:, r : r + 1]) * stats[:, 2 + r : 3 + r])
        mixed[r] = inputs + normed[r]

    height, size = 2 * rows, 8 * rows
    col_scale = 1.0 / math.sqrt(height)
    flat = jnp.concatenate([normed[0].astype(BF16), normed[1].astype(BF16)], axis=0)
    z1_send[...] = dot(tab[0], flat).reshape(rows, 8, C).astype(BF16)
    for r in staged_peers:
        send(z1_send.at[r], z1_recv.at[row], Z1, (r, grp))
    z1_recv[row] = z1_send[row]

    for g in g_peers:
        send(head, hw_recv.at[grp], HW, (row, g))
    send(now.at[:, pl.ds(8, 8)], halo_up, HUP, (row_below, grp))
    send(now.at[:, pl.ds(0, 8)], halo_down, HDN, (row_above, grp))
    lanes = now.shape[2]
    send(now.at[:, :, pl.ds(lanes - C, C)], halo_left, HLF, (row, lax.rem(grp + 1, groups)))
    send(now.at[:, :, pl.ds(0, C)], halo_right, HRT, (row, lax.rem(grp + groups - 1, groups)))
    loads["first"].wait()
    loads["second"].wait()
    weight_one = (complex_matrix(first) * col_scale).astype(BF16)
    weight_two, weight_two_lo = split_hi_lo(complex_matrix(second))
    loads["up"].wait()
    loads["down"].wait()
    loads["ice"].wait()
    for i in range(1, 4):
        loads["tab" + str(i)].wait()
    block_at = lax.broadcasted_iota(jnp.int32, (16, total_channels), 0) % 8
    block_of = lax.broadcasted_iota(jnp.int32, (16, total_channels), 1) // C
    pick = jnp.where(block_at == block_of, 1.0, 0.0).astype(BF16)

    def column_sums(weights):
        hi, lo = split_hi_lo(dot(pick, weights))
        return jnp.concatenate([hi[:16], lo, jnp.zeros((C - 32, weights.shape[1]), BF16)], axis=0)

    own_sums = column_sums(up[...])

    def blocks(values):
        return [values[i * height : (i + 1) * height] for i in range(4)]

    arrived(Z1, z1_recv.at[pl.ds(0, rows - 1)])
    columns = z1_recv[...].astype(F32).reshape(size, C).astype(BF16)
    freq = blocks(dot(tab[1], columns).astype(BF16))
    freq = jnp.concatenate(
        [jnp.concatenate(freq[:2], axis=1), jnp.concatenate(freq[2:], axis=1)], axis=0
    )
    hid = jax.nn.relu(dot(freq, weight_one)).astype(BF16)
    mix = soft_shrink(dot(hid, weight_two) + dot(hid, weight_two_lo)).astype(BF16)
    mix = jnp.concatenate(
        [mix[kk * height : (kk + 1) * height, p * C : (p + 1) * C] for kk in range(2) for p in range(2)], axis=0
    )
    z2_send[...] = (dot(tab[2], mix) * col_scale).reshape(rows, 8, C).astype(BF16)
    for r in r_peers:
        send(z2_send.at[r], z2_recv.at[row], Z2, (r, grp))
    z2_recv[row] = z2_send[row]

    arrived(Z2, z2_recv.at[pl.ds(0, rows - 1)])
    columns = z2_recv[...].astype(F32).reshape(size, C).astype(BF16)
    square_ones = jnp.ones((C, C), BF16)
    for r in range(2):
        values = mixed[r] + dot(tab[3, r * width : (r + 1) * width], columns)
        mixed[r] = values
        hi = values.astype(BF16)
        local_mean = dot(hi, square_ones) * (1.0 / C)
        centered = (values - local_mean).astype(BF16)
        y_send[r] = centered
        wide = centered.astype(F32)
        row_mean = dot_nt(ones, hi)[0:1] * (1.0 / C)
        row_sum = dot_nt(ones, centered)[0:1]
        sq_hi, sq_lo = split_hi_lo(wide * wide)
        row_square = (dot_nt(ones, sq_hi) + dot_nt(ones, sq_lo))[0:1]
        st2_send[r] = stack_halves([row_mean, row_sum, row_square], width)
    for g in g_peers:
        send(st2_send.at[g % 2], st2_recv.at[grp], ST2, (row, g))
    tile = width // groups
    cuts = (0, 1, 3, 5, 8) if groups == 8 else (0, groups // 2, groups)
    parts = range(len(cuts) - 1)
    for t in parts:
        tokens_at = pl.ds(cuts[t] * tile, (cuts[t + 1] - cuts[t]) * tile)
        for g in g_peers:
            send(y_send.at[g % 2, tokens_at], y_recv.at[grp, tokens_at], Y[t], (row, g))
    y_recv[grp] = y_send[side]
    st2_recv[grp] = st2_send[side]

    wait_on(recv_sem.at[WUP], peer_up.at[pl.ds(0, up.shape[0] // 2)])
    drains.append((WUP, peer_up.at[pl.ds(0, up.shape[0] // 2)]))
    send(peer_up.at[half_up], peer_up.at[half_up], FUP, sibling)
    wait_on(recv_sem.at[WDN], peer_down.at[pl.ds(0, hidden // 2)])
    drains.append((WDN, peer_down.at[pl.ds(0, hidden // 2)]))
    send(peer_down.at[half_dn], peer_down.at[half_dn], FDN, sibling)

    arrived(HW, hw_recv.at[pl.ds(0, groups - 1)])
    whole_head = hw_recv[...].reshape(total_channels, C)
    head_sums = column_sums(whole_head)
    own_head = dot(down[...], whole_head).astype(BF16)
    arrived(FUP, peer_up.at[pl.ds(0, up.shape[0] // 2)])
    peer_sums = column_sums(peer_up[...])
    arrived(FDN, peer_down.at[pl.ds(0, hidden // 2)])
    peer_head = dot(peer_down[...], whole_head).astype(BF16)
    arrived(ST2, st2_recv.at[pl.ds(0, groups - 1)])
    sent = [[whole_row(st2_recv[g], i) for i in range(3)] for g in range(groups)]
    mean = jnp.zeros((1, width), F32)
    for row_mean, row_sum, _ in sent:
        mean = mean + (row_mean + row_sum * (1.0 / C))
    mean = mean * (1.0 / groups)
    offsets = [row_mean - mean for row_mean, _, _ in sent]
    square = jnp.zeros((1, width), F32)
    for offset, (_, row_sum, row_square) in zip(offsets, sent):
        square = square + (row_square + 2.0 * offset * row_sum + float(C) * offset * offset)
    scale = lax.rsqrt(square / total_channels + epsilon)
    local_means = in_parts([row_mean for row_mean, _, _ in sent], width)
    offsets = in_parts(offsets, width)
    scale = columns_of([scale], width)[:, 0:1]

    other = weight_peer[1]
    for t in parts:
        rows_at = slice(cuts[t] * tile, cuts[t + 1] * tile)
        part = pl.ds(rows_at.start, rows_at.stop - rows_at.start)
        arrived(Y[t], y_recv.at[pl.ds(0, groups - 1), part])
        flat = jnp.concatenate([y_recv[g, rows_at] for g in range(groups)], axis=1)

        def hidden_of(weights, sums):
            shift = dot(offsets[rows_at], sums)
            return gelu((dot(flat, weights) + shift) * scale[rows_at]).astype(BF16)

        hid_own = hidden_of(up[...], own_sums)
        hid_peer = hidden_of(peer_up[...], peer_sums)

        partial = (dot(hid_own, down[...]) + dot(hid_peer, peer_down[...])).astype(BF16)
        velocity = dot(hid_own, own_head) + dot(hid_peer, peer_head)
        for g in range(groups):
            rs_send[g, rows_at] = partial[:, g * C : (g + 1) * C]
        tiles = range(cuts[t], cuts[t + 1])
        vf_send[tiles.start : tiles.stop] = velocity.astype(BF16).reshape(len(tiles), tile, C)
        for g in tiles:

            @pl.when(grp != g)
            def _():
                send(vf_send.at[g], vf_recv.at[grp], VF, (row, g))

        for i in range(1, groups // 2):
            pair = lax.rem(grp // 2 + i, groups // 2)
            for g in (2 * pair, 2 * pair + 1):
                send(rs_send.at[g, part], rs_recv.at[grp, part], RS, (row, g))
        send(rs_send.at[other, part], rs_recv.at[grp, part], RS, (row, other))
    vf_recv[grp] = vf_send[grp]

    mine_at = pl.ds(pl.multiple_of((grp // 2) * 2 * tile, 2 * tile), 2 * tile)
    flat = jnp.concatenate([y_recv[g, mine_at] for g in range(groups)], axis=1)
    means[...] = local_means
    velocity = dot(flat, whole_head) + dot(means[mine_at], head_sums)
    vm_send[...] = velocity.astype(BF16).reshape(2, tile, C)
    send(vm_send.at[1 - side], vm_recv.at[side], VM, (row, other))
    vm_recv[side] = vm_send[side]
    rs_recv[grp] = rs_send[grp]

    for at, halo in ((HUP, halo_up), (HDN, halo_down), (HLF, halo_left), (HRT, halo_right)):
        arrived(at, halo)
    tile_rows = now.shape[1]
    row_at = lax.broadcasted_iota(jnp.int32, (tile_rows, lanes), 0)
    lane_at = lax.broadcasted_iota(jnp.int32, (tile_rows, lanes), 1)
    own = [now[0], now[1]]
    base = []
    for comp in range(2):
        above = jnp.where(row == 0, 0.0, halo_up[comp, 7:8, :])
        below = jnp.where(row == rows - 1, 0.0, halo_down[comp, 0:1, :])
        left = jnp.where(grp == 0, 0.0, halo_left[comp, :, C - 1 : C])
        right = jnp.where(grp == groups - 1, 0.0, halo_right[comp, :, 0:1])
        center = own[comp]
        up_shift = jnp.where(row_at == tile_rows - 1, below, jnp.roll(center, -1, axis=0))
        down_shift = jnp.where(row_at == 0, above, jnp.roll(center, 1, axis=0))
        from_right = jnp.where(lane_at == lanes - 1, right, jnp.roll(center, -1, axis=1))
        from_left = jnp.where(lane_at == 0, left, jnp.roll(center, 1, axis=1))
        laplace = up_shift + down_shift + from_right + from_left - 4.0 * center
        rotated = own[1] if comp == 0 else -own[0]
        base.append(center + time_step * (coriolis * rotated + viscosity * laplace))

    arrived(VF, vf_recv.at[pl.ds(0, groups - 1)])
    arrived(VM, vm_recv.at[0])
    velocity = []
    for r in range(2):
        values = vm_recv[r].astype(F32)
        for g in range(r, groups, 2):
            values = values + vf_recv[g].astype(F32)
        velocity.append(values)
    velocity.append(jnp.zeros((C - 2 * tile, C), F32))
    velocity = jnp.concatenate(velocity, axis=0).T

    wide = 2 * lanes
    source = lax.broadcasted_iota(jnp.int32, (C, wide), 0)
    target = lax.broadcasted_iota(jnp.int32, (C, wide), 1) // PATCH
    spread = jnp.where(source == target, 1.0, 0.0).astype(BF16)
    vel_hi, vel_lo = split_hi_lo(velocity)
    spread_out = dot(vel_hi, spread) + dot(vel_lo, spread)
    x_row = lax.broadcasted_iota(jnp.int32, (C, wide), 0) % PATCH
    x_lane = lax.broadcasted_iota(jnp.int32, (C, wide), 1) % PATCH
    kept = jnp.where(x_row == x_lane, spread_out, 0.0).reshape(C // PATCH, PATCH, wide)
    cells = jnp.sum(kept, axis=1)
    relative = []
    for comp in range(2):
        part = cells[comp * PATCH : (comp + 1) * PATCH]
        ice_vel = jnp.concatenate([part[:, :lanes], part[:, lanes:]], axis=0)
        relative.append(ice_vel - own[comp])
    speed = jnp.sqrt(relative[0] * relative[0] + relative[1] * relative[1] + speed_floor)
    drag = (time_step * drag_coef) * ice[...].astype(F32) * speed
    open_water = land[...].astype(F32)
    for comp in range(2):
        ocean[comp] = open_water * (base[comp] + drag * relative[comp])
    out_copies = []
    ocean_copy = pltpu.make_async_copy(ocean, oc_hbm, out_sem.at[2])
    ocean_copy.start()

    arrived(RS, rs_recv.at[pl.ds(0, groups - 1)])
    for r in range(2):
        values = rs_recv[r].astype(F32)
        for g in range(r + 2, groups, 2):
            values = values + rs_recv[g].astype(F32)
        bo[r] = (mixed[r] + values).astype(BF16)
        out_copies.append(pltpu.make_async_copy(bo.at[r], bo_hbm.at[r], out_sem.at[r]))
        out_copies[r].start()

    for at, like in drains:
        wait_on(send_sem.at[at], like)
    for copy in out_copies + [ocean_copy]:
        copy.wait()


def in_parts(rows, width):
    top = stack_rows(rows, 8, width)
    values = jnp.concatenate([top, top, top, jnp.zeros((C - 24, width), F32)], axis=0).T
    hi, lo = split_hi_lo(values)
    lane = lax.broadcasted_iota(jnp.int32, values.shape, 1)
    return jnp.where((lane >= 8) & (lane < 16), lo.astype(F32), hi.astype(F32)).astype(BF16)


def quarters(ref):
    half = ref.shape[1] // 2
    return [ref.at[i, pl.ds(j * half, half)] for i in range(2) for j in range(2)]


def copy_kernel(bo_in, oc_in, bo_out, oc_out, bo, oc, sem):
    steps = list(zip(quarters(bo_in), quarters(bo), quarters(bo_out))) + [(oc_in, oc, oc_out)]
    loads = [pltpu.make_async_copy(src, mid, sem.at[0, i]) for i, (src, mid, _) in enumerate(steps)]
    stores = [pltpu.make_async_copy(mid, dst, sem.at[1, i]) for i, (_, mid, dst) in enumerate(steps)]
    for load in loads:
        load.start()
    for load, store in zip(loads, stores):
        load.wait()
        store.start()
    for store in stores:
        store.wait()


def body(tokens, spec_first, spec_second, up_weight, down_weight, head_weight, ocean_vel, land_mask, ice_mask):
    rows = lax.axis_size("row")
    groups = lax.axis_size("grp")
    _, width, _ = tokens.shape
    embed, hidden = up_weight.shape
    _, tile_rows, lanes = ocean_vel.shape
    tile = width // groups
    tables = jnp.asarray(dft_tables(rows))
    args = (
        tokens, spec_first, spec_second, up_weight, down_weight, head_weight, ocean_vel, land_mask, ice_mask, tables,
    )
    copies = [pltpu.VMEM(a.shape, a.dtype) for a in args]
    scratch = copies + [
        pltpu.VMEM((8, width // 2), F32),
        pltpu.VMEM((groups, 8, width // 2), F32),
        pltpu.VMEM((rows, 8, C), BF16),
        pltpu.VMEM((rows, 8, C), BF16),
        pltpu.VMEM((rows, 8, C), BF16),
        pltpu.VMEM((rows, 8, C), BF16),
        pltpu.VMEM((2, width, C), F32),
        pltpu.VMEM((2, width, C), BF16),
        pltpu.VMEM((groups, width, C), BF16),
        pltpu.VMEM((2, 8, width // 2), F32),
        pltpu.VMEM((groups, 8, width // 2), F32),
        pltpu.VMEM((embed, hidden), BF16),
        pltpu.VMEM((hidden, embed), BF16),
        pltpu.VMEM((groups, width, C), BF16),
        pltpu.VMEM((groups, width, C), BF16),
        pltpu.VMEM((2, width, C), BF16),
        pltpu.VMEM((width, C), BF16),
        pltpu.VMEM((2, tile, C), BF16),
        pltpu.VMEM((2, tile, C), BF16),
        pltpu.VMEM((groups, tile, C), BF16),
        pltpu.VMEM((groups, tile, C), BF16),
        pltpu.VMEM((groups, C, C), BF16),
        pltpu.VMEM((2, tile_rows, lanes), F32),
        pltpu.VMEM((2, 8, lanes), F32),
        pltpu.VMEM((2, 8, lanes), F32),
        pltpu.VMEM((2, tile_rows, C), F32),
        pltpu.VMEM((2, tile_rows, C), F32),
        pltpu.VMEM((2, tile_rows, lanes), F32),
        pltpu.SemaphoreType.DMA((len(args) + 3,)),
        pltpu.SemaphoreType.DMA((20,)),
        pltpu.SemaphoreType.DMA((20,)),
        pltpu.SemaphoreType.DMA((3,)),
    ]
    outs = (
        jax.ShapeDtypeStruct(tokens.shape, BF16),
        jax.ShapeDtypeStruct(ocean_vel.shape, F32),
    )
    results = pl.pallas_call(
        functools.partial(kernel, rows, groups),
        out_shape=outs,
        in_specs=[pl.BlockSpec(memory_space=pl.ANY)] * len(args),
        out_specs=[pl.BlockSpec(memory_space=pl.ANY)] * 2,
        scratch_shapes=scratch,
        compiler_params=pltpu.CompilerParams(
            collective_id=0, has_side_effects=True, vmem_limit_bytes=60 * 1024 * 1024
        ),
    )(*args)
    return pl.pallas_call(
        copy_kernel,
        out_shape=outs,
        in_specs=[pl.BlockSpec(memory_space=pl.ANY)] * 2,
        out_specs=[pl.BlockSpec(memory_space=pl.ANY)] * 2,
        scratch_shapes=[pltpu.VMEM(out.shape, out.dtype) for out in outs] + [pltpu.SemaphoreType.DMA((2, 5))],
    )(*results)


def solution(mesh):
    placed = (
        P("row", None, "grp"),
        P(None, "grp", None),
        P(None, "grp", None),
        P(None, "grp"),
        P("grp", None),
        P("grp", None),
        P(None, "row", "grp"),
        P("row", "grp"),
        P("row", "grp"),
    )
    return jax.shard_map(
        body,
        mesh=mesh,
        in_specs=placed,
        out_specs=(P("row", None, "grp"), P(None, "row", "grp")),
        check_vma=False,
    )
```
